128 devices in a mesh: chan: 32 (over z_lo, y, x), win: 4 (over z_hi, core).
Axes of the slice: x: 4, y: 4, z: 4 (z_hi: 2, z_lo: 2; z = z_hi * 2 + z_lo), core: 2. Of those that a mesh axis runs over, the one named last changes fastest.
Arguments:
- spectra: bfloat16 [2, 20, 512, 1536], P(None, 'win', 'chan'), may hold values from -40 to 40
- partners: int32 [512, 256], P('chan'), may hold values from 0 to 511, as said below
- pair_mask: int32 [512, 256], P('chan'), may hold values from 0 to 1, as said below
- gap_flags: int32 [512], P('chan'), may hold values 0 or 1
Outputs:
- lags: float32 [256, 512, 256], P('win', 'chan')
The draws below stay inside these ranges and needn't reach their ends.
Inputs may be any that keep to these rules, and one draw needn't show every extreme that they name: `partners`: the 256 slots of channel c hold the channels c + o for every offset o from -128 to 128 but 0, in an order drawn from the seed; a slot whose offset leaves the cable holds c itself. `pair_mask`: 1 exactly where the slot's offset is at most 100 in magnitude and its channel lies on the cable.
All inputs are finite; a program needn't handle non-finite values. No bound on the sum of `gap_flags` on one device may be relied on, other than what follows from the above.
Results may differ from the reference program's by a relative error of at most 0.0041.
Values may be sent and summed in bfloat16 or wider, within the bound.
A program may use at most 128 MiB of HBM per device.

```python
import math
import jax
import jax.numpy as jnp
from jax import lax

F = 1536
LAGS = 256
REACH = 128
SMOOTH = 8
FLO = 64
NSAMP = 6000
LIMIT = 100
CHANNELS = 512
W = 20


def pair_layout(key):
    layout_key = jax.random.fold_in(key, 7)
    offsets = jnp.concatenate([-jnp.arange(REACH, 0, -1, dtype=jnp.int32), jnp.arange(1, REACH + 1, dtype=jnp.int32)])
    ordered = jax.random.permutation(layout_key, jnp.broadcast_to(offsets, (CHANNELS, 2 * REACH)), axis=1, independent=True)
    channel = jnp.arange(CHANNELS, dtype=jnp.int32)[:, None]
    target = channel + ordered
    inside = (target >= 0) & (target < CHANNELS)
    valid = inside & (jnp.abs(ordered) <= LIMIT)
    return (jnp.where(inside, target, channel).astype(jnp.int32), valid.astype(jnp.int32))


def draw_partners(key, part):
    return pair_layout(key)[0]


def draw_pair_mask(key, part):
    return pair_layout(key)[1]


def draw_spectra(key, part):
    key = jax.random.fold_in(key, 3)
    noise_key, scale_key = jax.random.split(key, 2)
    shape = (2, W, CHANNELS, F)
    scale = jnp.exp(jax.random.uniform(scale_key, (1, W, CHANNELS, 1), jnp.float32, jnp.log(0.3), jnp.log(3.0)))
    values = jax.random.normal(noise_key, shape, jnp.float32) * scale
    return jnp.clip(values, -40.0, 40.0).astype(jnp.bfloat16)


def with_ends(drawn, key, least, top_value):
    dims = drawn.shape
    spot = [jax.random.randint(jax.random.fold_in(key, axis), (), 0, dims[axis]) for axis in range(len(dims))]
    drawn = drawn.at[tuple(spot)].set(least)
    longest = dims.index(max(dims))
    spot[longest] = (spot[longest] + 1) % dims[longest]
    return drawn.at[tuple(spot)].set(top_value)


def setup_inputs(seed: int = 0) -> dict:
    keys = jax.random.split(jax.random.key(seed), 5)
    spectra = draw_spectra(jax.random.fold_in(keys[4], 71), 0)
    partners = draw_partners(jax.random.fold_in(keys[4], 71), 0)
    pair_mask = draw_pair_mask(jax.random.fold_in(keys[4], 71), 0)
    gap_flags = with_ends((jax.random.randint(keys[3], (CHANNELS,), 0, 10) < 1).astype(jnp.int32), jax.random.fold_in(keys[3], 1), 0, 1)
    return dict(spectra=spectra, partners=partners, pair_mask=pair_mask, gap_flags=gap_flags)


water_level = 0.1

def whiten(spectra, gap_flags, half_width):
    real_part = spectra[0].astype(jnp.float32)
    imag_part = spectra[1].astype(jnp.float32)
    magnitude = jnp.sqrt(real_part * real_part + imag_part * imag_part)
    bins = magnitude.shape[-1]
    padded = jnp.pad(magnitude, ((0, 0), (0, 0), (half_width, half_width)))
    window_sum = padded[..., 0:bins]
    for offset_bin in range(1, 2 * half_width + 1):
        window_sum = window_sum + padded[..., offset_bin:offset_bin + bins]
    positions = jnp.arange(bins, dtype=jnp.int32)
    bin_count = (jnp.minimum(positions + half_width, bins - 1) - jnp.maximum(positions - half_width, 0) + 1).astype(jnp.float32)
    smooth = window_sum / bin_count
    band_mean = lax.optimization_barrier(jnp.mean(magnitude, axis=-1, keepdims=True))
    divisor = smooth + water_level * band_mean + 1e-06
    live_channel = (gap_flags == 0).astype(jnp.float32)[None, :, None]
    return jnp.stack([real_part / divisor * live_channel, imag_part / divisor * live_channel]).astype(jnp.bfloat16)

def lag_table(first_bin, bin_total, total_bins):
    bins = first_bin + jnp.arange(bin_total, dtype=jnp.int32)
    offsets = jnp.arange(LAGS, dtype=jnp.int32) - LAGS // 2
    phase_steps = jnp.mod((FLO + bins)[:, None] * offsets[None, :], NSAMP)
    angles = phase_steps.astype(jnp.float32) * (2.0 * math.pi / NSAMP)
    return jnp.concatenate([jnp.cos(angles), -jnp.sin(angles)], 0) / math.sqrt(total_bins)

def reference(spectra, partners, pair_mask, gap_flags):
    windows = spectra.shape[1]
    channels = spectra.shape[2]
    bins = spectra.shape[3]
    slots = partners.shape[1]
    reach_span = slots // 2
    whitened = whiten(spectra, gap_flags, SMOOTH)
    extended = jnp.pad(whitened, ((0, 0), (0, 0), (reach_span, reach_span), (0, 0)))
    basis = lag_table(0, bins, bins)
    slot_index = (partners + reach_span).astype(jnp.int32)
    weights = pair_mask.astype(jnp.float32) / math.sqrt(windows)
    group = 2

    def one_block(block_number):
        first_row = (block_number * group).astype(jnp.int32)
        rows = lax.dynamic_slice_in_dim(slot_index, first_row, group, 0)
        slot_weight = lax.dynamic_slice_in_dim(weights, first_row, group, 0)
        own_rows = lax.dynamic_slice_in_dim(whitened, first_row, group, 2).astype(jnp.float32)
        partner_rows = jnp.take(extended, rows.reshape(-1), axis=2).astype(jnp.float32)
        partner_rows = partner_rows.reshape(2, windows, group, slots, bins)
        cross_real = jnp.einsum('wcf,wcpf->cpf', own_rows[0], partner_rows[0]) + jnp.einsum('wcf,wcpf->cpf', own_rows[1], partner_rows[1])
        cross_imag = jnp.einsum('wcf,wcpf->cpf', own_rows[1], partner_rows[0]) - jnp.einsum('wcf,wcpf->cpf', own_rows[0], partner_rows[1])
        joined = jnp.concatenate([cross_real * slot_weight[:, :, None], cross_imag * slot_weight[:, :, None]], -1)
        joined = joined.reshape(group * slots, 2 * bins)
        result = jnp.dot(joined, basis, precision=lax.Precision.HIGHEST, preferred_element_type=jnp.float32)
        return result.reshape(group, slots, basis.shape[1])
    stacked = lax.map(one_block, jnp.arange(channels // group, dtype=jnp.int32))
    stacked = stacked.reshape(channels, slots, basis.shape[1])
    return jnp.transpose(stacked, (1, 0, 2))
```

```python
import math

import jax
import jax.numpy as jnp
import numpy as np
from jax import lax
from jax.experimental import pallas as pl
from jax.experimental.pallas import tpu as pltpu
from jax.sharding import PartitionSpec as P

LAGS = 256
SMOOTH = 8
FLO = 64
NSAMP = 6000
water_level = 0.1

MESH = pl.DeviceIdType.MESH
BLOCKS = 7
TILE = 128
SUB = 16
QUAD = 64
QUAD_LANES = 640
CHUNK = 256
CHUNK_LANES = CHUNK // QUAD * QUAD_LANES


def bin_order():
    main = np.zeros((8 * TILE, 8 * TILE), np.float32)
    part, f = np.meshgrid(np.arange(8), np.arange(TILE), indexing="ij")
    main[part * TILE + f, (f // SUB) * TILE + part * SUB + f % SUB] = 1.0
    rest = np.zeros((2 * TILE, 2 * TILE), np.float32)
    part, f = np.meshgrid(np.arange(2), np.arange(TILE), indexing="ij")
    rest[part * TILE + f, (f // QUAD) * TILE + part * QUAD + f % QUAD] = 1.0
    return main.astype(jnp.bfloat16), rest.astype(jnp.bfloat16)


def lag_tables(bins):
    steps = np.mod((FLO + np.arange(bins))[:, None] * (np.arange(LAGS) - LAGS // 2)[None, :], NSAMP)
    angles = steps.astype(np.float64) * (2.0 * math.pi / NSAMP)
    shape = (bins // CHUNK, CHUNK, LAGS)
    return (
        np.cos(angles).astype(np.float32).reshape(shape).astype(jnp.bfloat16),
        np.sin(angles).astype(np.float32).reshape(shape).astype(jnp.bfloat16),
    )


def whiten_kernel(spectra_ref, live_ref, main_ref, rest_ref, x_ref, y_ref, held):
    windows, channels, bins = spectra_ref.shape[1:]
    tiles = bins // TILE
    position = lax.broadcasted_iota(jnp.int32, (1, bins), 1)
    count = (jnp.minimum(position + SMOOTH, bins - 1) - jnp.maximum(position - SMOOTH, 0) + 1).astype(jnp.float32)
    live = live_ref[...]
    pad = jnp.zeros((channels, TILE), jnp.float32)
    for window in range(windows):
        real_part = spectra_ref[0, window].astype(jnp.float32)
        imag_part = spectra_ref[1, window].astype(jnp.float32)
        magnitude = jnp.sqrt(real_part * real_part + imag_part * imag_part)
        band_mean = jnp.sum(magnitude, axis=1, keepdims=True) * (1.0 / bins)
        padded = jnp.concatenate([magnitude, pad], axis=1)
        width = bins + TILE
        total = padded
        for step in (1, 2, 4, 8):
            total = total + pltpu.roll(total, step, 1)
        around = pltpu.roll(total, width - SMOOTH, 1) + pltpu.roll(padded, SMOOTH, 1)
        divisor = around[:, :bins] / count + water_level * band_mean + 1e-06
        white_real = (real_part / divisor * live).astype(jnp.bfloat16)
        white_imag = (imag_part / divisor * live).astype(jnp.bfloat16)
        minus_real = -white_real
        for tile in range(tiles):
            rows = slice(tile * channels, (tile + 1) * channels)
            lanes = slice(tile * TILE, (tile + 1) * TILE)
            first = slice(2 * window * TILE, (2 * window + 1) * TILE)
            second = slice((2 * window + 1) * TILE, (2 * window + 2) * TILE)
            held[0, rows, first] = white_real[:, lanes]
            held[0, rows, second] = white_imag[:, lanes]
            held[1, rows, first] = white_imag[:, lanes]
            held[1, rows, second] = minus_real[:, lanes]
    for which, out_ref in ((0, x_ref), (1, y_ref)):
        main = jnp.dot(held[which, :, : 8 * TILE], main_ref[...], preferred_element_type=jnp.float32)
        rest = jnp.dot(held[which, :, 8 * TILE :], rest_ref[...], preferred_element_type=jnp.float32)
        main = main.astype(jnp.bfloat16)
        rest = rest.astype(jnp.bfloat16)
        for tile in range(tiles):
            rows = slice(tile * channels, (tile + 1) * channels)
            for half in range(2):
                quad = tile * 2 + half
                chunk, start = quad // (CHUNK // QUAD), quad % (CHUNK // QUAD) * QUAD_LANES
                out_ref[chunk, :, start : start + 4 * TILE] = main[rows, half * 4 * TILE : (half + 1) * 4 * TILE]
                out_ref[chunk, :, start + 4 * TILE : start + QUAD_LANES] = rest[rows, half * TILE : (half + 1) * TILE]


def stack_kernel(
    x_ref, y_ref, cos_ref, sin_ref, rel_ref, out_ref,
    around, cross, even, odd, ahead, back_out, back_in, picked, from_core, to_far, from_far,
    halo_send, halo_recv, back_send, back_recv, core_send, core_recv, far_send, far_recv,
):
    chunks, channels = x_ref.shape[:2]
    span = around.shape[1]
    count = lax.axis_size("chan")
    me = lax.axis_index("chan")
    win = lax.axis_index("win")
    core = lax.rem(win, 2)
    far = win // 2
    other_core = win + 1 - 2 * core
    other_far = lax.rem(win + 2, 4)

    def above(distance):
        return lax.rem(me + distance, count)

    def below(distance):
        return lax.rem(me + count - distance, count)

    barrier = pltpu.get_barrier_semaphore()
    for distance in range(1, BLOCKS + 1):
        for chan in (above(distance), below(distance)):
            pl.semaphore_signal(barrier, inc=1, device_id={"chan": chan, "win": win}, device_id_type=MESH)
    for partner in (other_core, other_far):
        pl.semaphore_signal(barrier, inc=1, device_id={"chan": me, "win": partner}, device_id_type=MESH)
    pl.semaphore_wait(barrier, 2 * BLOCKS + 2)

    def halo(chunk, distance):
        return pltpu.make_async_remote_copy(
            src_ref=x_ref.at[chunk],
            dst_ref=around.at[chunk, pl.ds(distance * channels, channels), :],
            send_sem=halo_send.at[chunk, distance - 1],
            recv_sem=halo_recv.at[chunk, distance - 1],
            device_id={"chan": below(distance), "win": win},
            device_id_type=MESH,
        )

    for chunk in range(chunks):
        for distance in range(1, BLOCKS + 1):
            halo(chunk, distance).start()
    for chunk in range(chunks):
        around[chunk, :channels, :] = x_ref[chunk]
    even[...] = jnp.zeros_like(even)
    odd[...] = jnp.zeros_like(odd)

    row = lax.broadcasted_iota(jnp.int32, (SUB, TILE), 0)
    lane = lax.broadcasted_iota(jnp.int32, (SUB, TILE), 1)
    masks = []
    for group in range(QUAD // SUB):
        main = (lane % SUB == row).astype(jnp.float32)
        rest = (lane % QUAD == group * SUB + row).astype(jnp.float32)
        masks.append(jnp.concatenate([main, rest], axis=1).astype(jnp.bfloat16))

    def one_chunk(chunk, _):
        for distance in range(1, BLOCKS + 1):
            halo(chunk, distance).wait_recv()

        def one_quad(quad, _):
            start = pl.multiple_of(quad * QUAD_LANES, TILE)

            def tiles(ref, group):
                first = ref[chunk, :, pl.ds(pl.multiple_of(start + group * TILE, TILE), TILE)]
                last = ref[chunk, :, pl.ds(pl.multiple_of(start + 4 * TILE, TILE), TILE)]
                return jnp.concatenate([first, last], axis=1)

            for group in range(QUAD // SUB):
                partners = tiles(around, group)
                for part, ref in ((0, x_ref), (1, y_ref)):
                    own = tiles(ref, group)
                    spread = (own[:, None, :] * masks[group][None, :, :]).reshape(channels * SUB, 2 * TILE)
                    product = lax.dot_general(
                        spread, partners, (((1,), (1,)), ((), ())), preferred_element_type=jnp.float32
                    )
                    first_bin = pl.multiple_of(quad * QUAD + group * SUB, SUB)
                    cross[part, :, pl.ds(first_bin, SUB), :] = product.astype(jnp.bfloat16).reshape(channels, SUB, span)
            return 0

        lax.fori_loop(0, CHUNK // QUAD, one_quad, 0)

        def one_channel(channel, _):
            for part, table, total in ((0, cos_ref, even), (1, sin_ref, odd)):
                total[channel] += lax.dot_general(
                    cross[part, channel], table[chunk], (((0,), (0,)), ((), ())), preferred_element_type=jnp.float32
                )
            return 0

        lax.fori_loop(0, channels, one_channel, 0)
        return 0

    lax.fori_loop(0, chunks, one_chunk, 0)

    def lags_of(channel, _):
        cos_sum = even[channel]
        sin_sum = odd[channel]
        ahead[channel] = (cos_sum - sin_sum).astype(jnp.bfloat16)
        mirrored = (cos_sum + sin_sum).astype(jnp.bfloat16)
        for distance in range(1, BLOCKS + 1):
            back_out[distance - 1, channel] = mirrored[distance * channels : (distance + 1) * channels]
        return 0

    lax.fori_loop(0, channels, lags_of, 0)

    def back(distance):
        return pltpu.make_async_remote_copy(
            src_ref=back_out.at[distance - 1],
            dst_ref=back_in.at[distance - 1],
            send_sem=back_send.at[distance - 1],
            recv_sem=back_recv.at[distance - 1],
            device_id={"chan": above(distance), "win": win},
            device_id_type=MESH,
        )

    for distance in range(1, BLOCKS + 1):
        back(distance).start()
    for distance in range(1, BLOCKS + 1):
        back(distance).wait_recv()

    slots = rel_ref.shape[1]

    def pick(channel, _):
        target = rel_ref[channel]
        lanes = lax.broadcasted_iota(jnp.int32, (slots, span), 1)
        chosen = (lanes == target).astype(jnp.float32).astype(jnp.bfloat16)
        total = jnp.dot(chosen, ahead[channel], preferred_element_type=jnp.float32)
        lanes = lax.broadcasted_iota(jnp.int32, (slots, channels * channels), 1)
        for distance in range(1, BLOCKS + 1):
            place = (target + distance * channels) * channels + channel
            chosen = (lanes == place).astype(jnp.float32).astype(jnp.bfloat16)
            rows = back_in[distance - 1].reshape(channels * channels, LAGS)
            total += jnp.dot(chosen, rows, preferred_element_type=jnp.float32)
        picked[channel] = total.astype(jnp.bfloat16)
        return 0

    lax.fori_loop(0, channels, pick, 0)

    share = slots // 4

    def slots_of(owner):
        return pl.ds(pl.multiple_of(owner * share, share), share)

    def to_core(half):
        return pltpu.make_async_remote_copy(
            src_ref=picked.at[:, slots_of(2 * half + 1 - core), :],
            dst_ref=from_core.at[half],
            send_sem=core_send.at[half],
            recv_sem=core_recv.at[half],
            device_id={"chan": me, "win": other_core},
            device_id_type=MESH,
        )

    for half in range(2):
        to_core(half).start()
    for half in range(2):
        to_core(half).wait_recv()

    def far_sum(channel, _):
        mine = picked[channel, slots_of(other_far), :].astype(jnp.float32)
        to_far[channel] = (mine + from_core[1 - far, channel].astype(jnp.float32)).astype(jnp.bfloat16)
        return 0

    lax.fori_loop(0, channels, far_sum, 0)
    away = pltpu.make_async_remote_copy(
        src_ref=to_far,
        dst_ref=from_far,
        send_sem=far_send,
        recv_sem=far_recv,
        device_id={"chan": me, "win": other_far},
        device_id_type=MESH,
    )
    away.start()
    away.wait_recv()

    def last_sum(channel, _):
        mine = picked[channel, slots_of(win), :].astype(jnp.float32)
        out_ref[channel] = (
            mine + from_core[far, channel].astype(jnp.float32) + from_far[channel].astype(jnp.float32)
        )
        return 0

    lax.fori_loop(0, channels, last_sum, 0)

    for chunk in range(chunks):
        for distance in range(1, BLOCKS + 1):
            halo(chunk, distance).wait_send()
    for distance in range(1, BLOCKS + 1):
        back(distance).wait_send()
    for half in range(2):
        to_core(half).wait_send()
    away.wait_send()


def on_device(spectra, partners, pair_mask, gap_flags):
    _, windows, channels, bins = spectra.shape
    slots = partners.shape[1]
    chunks = bins // CHUNK
    span = (BLOCKS + 1) * channels
    share = slots // 4
    bf16 = jnp.bfloat16
    whole = pl.BlockSpec(memory_space=pltpu.VMEM)
    main, rest = bin_order()
    cos_table, sin_table = lag_tables(bins)
    live = (gap_flags == 0).astype(jnp.float32)[:, None]
    own = jax.ShapeDtypeStruct((chunks, channels, CHUNK_LANES), bf16)
    x, y = pl.pallas_call(
        whiten_kernel,
        out_shape=(own, own),
        in_specs=[whole] * 4,
        out_specs=(whole, whole),
        scratch_shapes=[pltpu.VMEM((2, bins // TILE * channels, 2 * windows * TILE), bf16)],
        compiler_params=pltpu.CompilerParams(vmem_limit_bytes=40 * 2**20),
        name="whiten",
    )(spectra, live, main, rest)

    first = lax.axis_index("chan") * channels
    rel = jnp.where(pair_mask > 0, partners - first, -(2**20))[:, :, None]
    stacked = pl.pallas_call(
        stack_kernel,
        out_shape=jax.ShapeDtypeStruct((channels, share, LAGS), jnp.float32),
        in_specs=[whole] * 5,
        out_specs=whole,
        scratch_shapes=[
            pltpu.VMEM((chunks, span, CHUNK_LANES), bf16),
            pltpu.VMEM((2, channels, CHUNK, span), bf16),
            pltpu.VMEM((channels, span, LAGS), jnp.float32),
            pltpu.VMEM((channels, span, LAGS), jnp.float32),
            pltpu.VMEM((channels, span, LAGS), bf16),
            pltpu.VMEM((BLOCKS, channels, channels, LAGS), bf16),
            pltpu.VMEM((BLOCKS, channels, channels, LAGS), bf16),
            pltpu.VMEM((channels, slots, LAGS), bf16),
            pltpu.VMEM((2, channels, share, LAGS), bf16),
            pltpu.VMEM((channels, share, LAGS), bf16),
            pltpu.VMEM((channels, share, LAGS), bf16),
            pltpu.SemaphoreType.DMA((chunks, BLOCKS)),
            pltpu.SemaphoreType.DMA((chunks, BLOCKS)),
            pltpu.SemaphoreType.DMA((BLOCKS,)),
            pltpu.SemaphoreType.DMA((BLOCKS,)),
            pltpu.SemaphoreType.DMA((2,)),
            pltpu.SemaphoreType.DMA((2,)),
            pltpu.SemaphoreType.DMA,
            pltpu.SemaphoreType.DMA,
        ],
        compiler_params=pltpu.CompilerParams(
            collective_id=0, has_side_effects=True, vmem_limit_bytes=56 * 2**20
        ),
        name="stack",
    )(x, y, cos_table, sin_table, rel)
    scale = 1.0 / math.sqrt(windows * lax.axis_size("win") * bins)
    return jnp.transpose(stacked, (1, 0, 2)) * scale


def solution(mesh):
    placed = (P(None, "win", "chan", None), P("chan", None), P("chan", None), P("chan"))
    return jax.shard_map(
        on_device, mesh=mesh, in_specs=placed, out_specs=P("win", "chan", None), check_vma=False
    )
```

```python
import math

import jax
import jax.numpy as jnp
import numpy as np
from jax import lax
from jax.experimental import pallas as pl
from jax.experimental.pallas import tpu as pltpu
from jax.sharding import PartitionSpec as P

LAGS = 256
SMOOTH = 8
FLO = 64
NSAMP = 6000
water_level = 0.1

MESH = pl.DeviceIdType.MESH
OFFSETS = (1, -2, 3, -4, 5, -6, 7)
BLOCKS = len(OFFSETS)
TILE = 128
SUB = 16
QUAD = 64
QUAD_LANES = 640
CHUNK = 256
CHUNK_LANES = CHUNK // QUAD * QUAD_LANES


def bin_order():
    main = np.zeros((8 * TILE, 8 * TILE), np.float32)
    part, f = np.meshgrid(np.arange(8), np.arange(TILE), indexing="ij")
    main[part * TILE + f, (f // SUB) * TILE + part * SUB + f % SUB] = 1.0
    rest = np.zeros((2 * TILE, 2 * TILE), np.float32)
    part, f = np.meshgrid(np.arange(2), np.arange(TILE), indexing="ij")
    rest[part * TILE + f, (f // QUAD) * TILE + part * QUAD + f % QUAD] = 1.0
    return main.astype(jnp.bfloat16), rest.astype(jnp.bfloat16)


def lag_tables(bins):
    steps = np.mod((FLO + np.arange(bins))[:, None] * (np.arange(LAGS) - LAGS // 2)[None, :], NSAMP)
    angles = steps.astype(np.float64) * (2.0 * math.pi / NSAMP)
    shape = (bins // CHUNK, CHUNK, LAGS)
    return (
        np.cos(angles).astype(np.float32).reshape(shape).astype(jnp.bfloat16),
        np.sin(angles).astype(np.float32).reshape(shape).astype(jnp.bfloat16),
    )


def whiten_kernel(spectra_ref, live_ref, main_ref, rest_ref, x_ref, y_ref, held):
    windows, channels, bins = spectra_ref.shape[1:]
    tiles = bins // TILE
    position = lax.broadcasted_iota(jnp.int32, (1, bins), 1)
    count = (jnp.minimum(position + SMOOTH, bins - 1) - jnp.maximum(position - SMOOTH, 0) + 1).astype(jnp.float32)
    live = live_ref[...]
    pad = jnp.zeros((channels, TILE), jnp.float32)
    for window in range(windows):
        real_part = spectra_ref[0, window].astype(jnp.float32)
        imag_part = spectra_ref[1, window].astype(jnp.float32)
        magnitude = jnp.sqrt(real_part * real_part + imag_part * imag_part)
        band_mean = jnp.sum(magnitude, axis=1, keepdims=True) * (1.0 / bins)
        padded = jnp.concatenate([magnitude, pad], axis=1)
        width = bins + TILE
        total = padded
        for step in (1, 2, 4, 8):
            total = total + pltpu.roll(total, step, 1)
        around = pltpu.roll(total, width - SMOOTH, 1) + pltpu.roll(padded, SMOOTH, 1)
        divisor = around[:, :bins] / count + water_level * band_mean + 1e-06
        white_real = (real_part / divisor * live).astype(jnp.bfloat16)
        white_imag = (imag_part / divisor * live).astype(jnp.bfloat16)
        minus_real = -white_real
        for tile in range(tiles):
            rows = slice(tile * channels, (tile + 1) * channels)
            lanes = slice(tile * TILE, (tile + 1) * TILE)
            first = slice(2 * window * TILE, (2 * window + 1) * TILE)
            second = slice((2 * window + 1) * TILE, (2 * window + 2) * TILE)
            held[0, rows, first] = white_real[:, lanes]
            held[0, rows, second] = white_imag[:, lanes]
            held[1, rows, first] = white_imag[:, lanes]
            held[1, rows, second] = minus_real[:, lanes]
    for which, out_ref in ((0, x_ref), (1, y_ref)):
        main = jnp.dot(held[which, :, : 8 * TILE], main_ref[...], preferred_element_type=jnp.float32)
        rest = jnp.dot(held[which, :, 8 * TILE :], rest_ref[...], preferred_element_type=jnp.float32)
        main = main.astype(jnp.bfloat16)
        rest = rest.astype(jnp.bfloat16)
        for tile in range(tiles):
            rows = slice(tile * channels, (tile + 1) * channels)
            for half in range(2):
                quad = tile * 2 + half
                chunk, start = quad // (CHUNK // QUAD), quad % (CHUNK // QUAD) * QUAD_LANES
                out_ref[chunk, :, start : start + 4 * TILE] = main[rows, half * 4 * TILE : (half + 1) * 4 * TILE]
                out_ref[chunk, :, start + 4 * TILE : start + QUAD_LANES] = rest[rows, half * TILE : (half + 1) * TILE]


def stack_kernel(
    x_ref, y_ref, cos_ref, sin_ref, rel_ref, out_ref,
    around, cross, even, odd, ahead, back_out, back_in, picked, from_core, to_far, from_far,
    halo_send, halo_recv, back_send, back_recv, core_send, core_recv, far_send, far_recv,
):
    chunks, channels = x_ref.shape[:2]
    span = around.shape[1]
    count = lax.axis_size("chan")
    me = lax.axis_index("chan")
    win = lax.axis_index("win")
    core = lax.rem(win, 2)
    far = win // 2
    other_core = win + 1 - 2 * core
    other_far = lax.rem(win + 2, 4)

    def block(offset):
        return lax.rem(me + count + offset, count)

    barrier = pltpu.get_barrier_semaphore()
    for offset in OFFSETS:
        for chan in (block(offset), block(-offset)):
            pl.semaphore_signal(barrier, inc=1, device_id={"chan": chan, "win": win}, device_id_type=MESH)
    for partner in (other_core, other_far):
        pl.semaphore_signal(barrier, inc=1, device_id={"chan": me, "win": partner}, device_id_type=MESH)
    pl.semaphore_wait(barrier, 2 * BLOCKS + 2)

    def halo(chunk, place):
        return pltpu.make_async_remote_copy(
            src_ref=x_ref.at[chunk],
            dst_ref=around.at[chunk, pl.ds((place + 1) * channels, channels), :],
            send_sem=halo_send.at[chunk, place],
            recv_sem=halo_recv.at[chunk, place],
            device_id={"chan": block(-OFFSETS[place]), "win": win},
            device_id_type=MESH,
        )

    for chunk in range(chunks):
        for place in range(BLOCKS):
            halo(chunk, place).start()
    for chunk in range(chunks):
        around[chunk, :channels, :] = x_ref[chunk]
    even[...] = jnp.zeros_like(even)
    odd[...] = jnp.zeros_like(odd)

    row = lax.broadcasted_iota(jnp.int32, (SUB, TILE), 0)
    lane = lax.broadcasted_iota(jnp.int32, (SUB, TILE), 1)
    masks = []
    for group in range(QUAD // SUB):
        main = (lane % SUB == row).astype(jnp.float32)
        rest = (lane % QUAD == group * SUB + row).astype(jnp.float32)
        masks.append(jnp.concatenate([main, rest], axis=1).astype(jnp.bfloat16))

    def one_chunk(chunk, _):
        for place in range(BLOCKS):
            halo(chunk, place).wait_recv()

        def one_quad(quad, _):
            start = pl.multiple_of(quad * QUAD_LANES, TILE)

            def tiles(ref, group):
                first = ref[chunk, :, pl.ds(pl.multiple_of(start + group * TILE, TILE), TILE)]
                last = ref[chunk, :, pl.ds(pl.multiple_of(start + 4 * TILE, TILE), TILE)]
                return jnp.concatenate([first, last], axis=1)

            for group in range(QUAD // SUB):
                partners = tiles(around, group)
                for part, ref in ((0, x_ref), (1, y_ref)):
                    own = tiles(ref, group)
                    spread = (own[:, None, :] * masks[group][None, :, :]).reshape(channels * SUB, 2 * TILE)
                    product = lax.dot_general(
                        spread, partners, (((1,), (1,)), ((), ())), preferred_element_type=jnp.float32
                    )
                    first_bin = pl.multiple_of(quad * QUAD + group * SUB, SUB)
                    cross[part, :, pl.ds(first_bin, SUB), :] = product.astype(jnp.bfloat16).reshape(channels, SUB, span)
            return 0

        lax.fori_loop(0, CHUNK // QUAD, one_quad, 0)

        def one_channel(channel, _):
            for part, table, total in ((0, cos_ref, even), (1, sin_ref, odd)):
                total[channel] += lax.dot_general(
                    cross[part, channel], table[chunk], (((0,), (0,)), ((), ())), preferred_element_type=jnp.float32
                )
            return 0

        lax.fori_loop(0, channels, one_channel, 0)
        return 0

    lax.fori_loop(0, chunks, one_chunk, 0)

    def lags_of(channel, _):
        cos_sum = even[channel]
        sin_sum = odd[channel]
        ahead[channel] = (cos_sum - sin_sum).astype(jnp.bfloat16)
        mirrored = (cos_sum + sin_sum).astype(jnp.bfloat16)
        for place in range(BLOCKS):
            back_out[place, channel] = mirrored[(place + 1) * channels : (place + 2) * channels]
        return 0

    lax.fori_loop(0, channels, lags_of, 0)

    def back(place):
        return pltpu.make_async_remote_copy(
            src_ref=back_out.at[place],
            dst_ref=back_in.at[place],
            send_sem=back_send.at[place],
            recv_sem=back_recv.at[place],
            device_id={"chan": block(OFFSETS[place]), "win": win},
            device_id_type=MESH,
        )

    for place in range(BLOCKS):
        back(place).start()
    for place in range(BLOCKS):
        back(place).wait_recv()

    slots = rel_ref.shape[1]

    lane = lax.broadcasted_iota(jnp.int32, (1, span), 1)
    held = lane
    for place, offset in enumerate(OFFSETS):
        held = jnp.where(lane // channels == place + 1, lane + (offset - place - 1) * channels, held)

    def pick(channel, _):
        target = rel_ref[channel]
        lanes = jnp.broadcast_to(held, (slots, span))
        chosen = (lanes == target).astype(jnp.float32).astype(jnp.bfloat16)
        total = jnp.dot(chosen, ahead[channel], preferred_element_type=jnp.float32)
        lanes = lax.broadcasted_iota(jnp.int32, (slots, channels * channels), 1)
        for place in range(BLOCKS):
            wanted = (target + OFFSETS[place] * channels) * channels + channel
            chosen = (lanes == wanted).astype(jnp.float32).astype(jnp.bfloat16)
            rows = back_in[place].reshape(channels * channels, LAGS)
            total += jnp.dot(chosen, rows, preferred_element_type=jnp.float32)
        picked[channel] = total.astype(jnp.bfloat16)
        return 0

    lax.fori_loop(0, channels, pick, 0)

    share = slots // 4

    def slots_of(owner):
        return pl.ds(pl.multiple_of(owner * share, share), share)

    def to_core(half):
        return pltpu.make_async_remote_copy(
            src_ref=picked.at[:, slots_of(2 * half + 1 - core), :],
            dst_ref=from_core.at[half],
            send_sem=core_send.at[half],
            recv_sem=core_recv.at[half],
            device_id={"chan": me, "win": other_core},
            device_id_type=MESH,
        )

    for half in range(2):
        to_core(half).start()
    for half in range(2):
        to_core(half).wait_recv()

    def far_sum(channel, _):
        mine = picked[channel, slots_of(other_far), :].astype(jnp.float32)
        to_far[channel] = (mine + from_core[1 - far, channel].astype(jnp.float32)).astype(jnp.bfloat16)
        return 0

    lax.fori_loop(0, channels, far_sum, 0)
    away = pltpu.make_async_remote_copy(
        src_ref=to_far,
        dst_ref=from_far,
        send_sem=far_send,
        recv_sem=far_recv,
        device_id={"chan": me, "win": other_far},
        device_id_type=MESH,
    )
    away.start()
    away.wait_recv()

    def last_sum(channel, _):
        mine = picked[channel, slots_of(win), :].astype(jnp.float32)
        out_ref[channel] = (
            mine + from_core[far, channel].astype(jnp.float32) + from_far[channel].astype(jnp.float32)
        )
        return 0

    lax.fori_loop(0, channels, last_sum, 0)

    for chunk in range(chunks):
        for place in range(BLOCKS):
            halo(chunk, place).wait_send()
    for place in range(BLOCKS):
        back(place).wait_send()
    for half in range(2):
        to_core(half).wait_send()
    away.wait_send()


def on_device(spectra, partners, pair_mask, gap_flags):
    _, windows, channels, bins = spectra.shape
    slots = partners.shape[1]
    chunks = bins // CHUNK
    span = (BLOCKS + 1) * channels
    share = slots // 4
    bf16 = jnp.bfloat16
    whole = pl.BlockSpec(memory_space=pltpu.VMEM)
    main, rest = bin_order()
    cos_table, sin_table = lag_tables(bins)
    live = (gap_flags == 0).astype(jnp.float32)[:, None]
    own = jax.ShapeDtypeStruct((chunks, channels, CHUNK_LANES), bf16)
    x, y = pl.pallas_call(
        whiten_kernel,
        out_shape=(own, own),
        in_specs=[whole] * 4,
        out_specs=(whole, whole),
        scratch_shapes=[pltpu.VMEM((2, bins // TILE * channels, 2 * windows * TILE), bf16)],
        compiler_params=pltpu.CompilerParams(vmem_limit_bytes=40 * 2**20),
        name="whiten",
    )(spectra, live, main, rest)

    first = lax.axis_index("chan") * channels
    rel = jnp.where(pair_mask > 0, partners - first, -(2**20))[:, :, None]
    stacked = pl.pallas_call(
        stack_kernel,
        out_shape=jax.ShapeDtypeStruct((channels, share, LAGS), jnp.float32),
        in_specs=[whole] * 5,
        out_specs=whole,
        scratch_shapes=[
            pltpu.VMEM((chunks, span, CHUNK_LANES), bf16),
            pltpu.VMEM((2, channels, CHUNK, span), bf16),
            pltpu.VMEM((channels, span, LAGS), jnp.float32),
            pltpu.VMEM((channels, span, LAGS), jnp.float32),
            pltpu.VMEM((channels, span, LAGS), bf16),
            pltpu.VMEM((BLOCKS, channels, channels, LAGS), bf16),
            pltpu.VMEM((BLOCKS, channels, channels, LAGS), bf16),
            pltpu.VMEM((channels, slots, LAGS), bf16),
            pltpu.VMEM((2, channels, share, LAGS), bf16),
            pltpu.VMEM((channels, share, LAGS), bf16),
            pltpu.VMEM((channels, share, LAGS), bf16),
            pltpu.SemaphoreType.DMA((chunks, BLOCKS)),
            pltpu.SemaphoreType.DMA((chunks, BLOCKS)),
            pltpu.SemaphoreType.DMA((BLOCKS,)),
            pltpu.SemaphoreType.DMA((BLOCKS,)),
            pltpu.SemaphoreType.DMA((2,)),
            pltpu.SemaphoreType.DMA((2,)),
            pltpu.SemaphoreType.DMA,
            pltpu.SemaphoreType.DMA,
        ],
        compiler_params=pltpu.CompilerParams(
            collective_id=0, has_side_effects=True, vmem_limit_bytes=56 * 2**20
        ),
        name="stack",
    )(x, y, cos_table, sin_table, rel)
    scale = 1.0 / math.sqrt(windows * lax.axis_size("win") * bins)
    return jnp.transpose(stacked, (1, 0, 2)) * scale


def solution(mesh):
    placed = (P(None, "win", "chan", None), P("chan", None), P("chan", None), P("chan"))
    return jax.shard_map(
        on_device, mesh=mesh, in_specs=placed, out_specs=P("win", "chan", None), check_vma=False
    )
```

```python
import math

import jax
import jax.numpy as jnp
import numpy as np
from jax import lax
from jax.experimental import pallas as pl
from jax.experimental.pallas import tpu as pltpu
from jax.sharding import PartitionSpec as P

LAGS = 256
SMOOTH = 8
FLO = 64
NSAMP = 6000
water_level = 0.1

MESH = pl.DeviceIdType.MESH
OFFSETS = (1, -2, 3, -4, 5, -6, 7)
BLOCKS = len(OFFSETS)
TILE = 128
SUB = 16
QUAD = 64
QUAD_LANES = 640
CHUNK = 256
CHUNK_LANES = CHUNK // QUAD * QUAD_LANES
GROUPS = 4
ABREAST = 4


def bin_order():
    main = np.zeros((8 * TILE, 8 * TILE), np.float32)
    part, f = np.meshgrid(np.arange(8), np.arange(TILE), indexing="ij")
    main[part * TILE + f, (f // SUB) * TILE + part * SUB + f % SUB] = 1.0
    rest = np.zeros((2 * TILE, 2 * TILE), np.float32)
    part, f = np.meshgrid(np.arange(2), np.arange(TILE), indexing="ij")
    rest[part * TILE + f, (f // QUAD) * TILE + part * QUAD + f % QUAD] = 1.0
    return main.astype(jnp.bfloat16), rest.astype(jnp.bfloat16)


def lag_tables(bins):
    steps = np.mod((FLO + np.arange(bins))[:, None] * (np.arange(LAGS) - LAGS // 2)[None, :], NSAMP)
    angles = steps.astype(np.float64) * (2.0 * math.pi / NSAMP)
    shape = (bins // CHUNK, CHUNK, LAGS)
    return (
        np.cos(angles).astype(np.float32).reshape(shape).astype(jnp.bfloat16),
        np.sin(angles).astype(np.float32).reshape(shape).astype(jnp.bfloat16),
    )


def kernel(
    spectra_ref, partners_ref, mask_ref, gap_ref, main_ref, rest_ref, cos_ref, sin_ref, out_ref,
    spectra, partners, mask, main, rest, cos_table, sin_table,
    held, turned, around, cross, even, odd, chosen, mirrored, lags, back_out, picked, from_core, to_far, from_far,
    load_sem, halo_send, halo_recv, back_send, back_recv, core_send, core_recv, far_send, far_recv,
):
    windows, channels, bins = spectra.shape[1:]
    tiles = bins // TILE
    chunks = bins // CHUNK
    span = around.shape[1]
    slots = partners.shape[1]
    share = slots // 4
    few = channels // GROUPS
    count = lax.axis_size("chan")
    me = lax.axis_index("chan")
    win = lax.axis_index("win")
    core = lax.rem(win, 2)
    far = win // 2
    other_core = win + 1 - 2 * core
    other_far = lax.rem(win + 2, 4)

    def block(offset):
        return lax.rem(me + count + offset, count)

    loads = [(spectra_ref.at[:, window], spectra.at[:, window]) for window in range(windows)]
    loads += [(main_ref, main), (rest_ref, rest), (partners_ref, partners), (mask_ref, mask)]
    loads += [(cos_ref, cos_table), (sin_ref, sin_table)]
    loads = [pltpu.make_async_copy(source, target, load_sem.at[i]) for i, (source, target) in enumerate(loads)]
    for load in loads:
        load.start()
    barrier = pltpu.get_barrier_semaphore()
    for offset in OFFSETS:
        for chan in (block(offset), block(-offset)):
            pl.semaphore_signal(barrier, inc=1, device_id={"chan": chan, "win": win}, device_id_type=MESH)
    for partner in (other_core, other_far):
        pl.semaphore_signal(barrier, inc=1, device_id={"chan": me, "win": partner}, device_id_type=MESH)

    position = lax.broadcasted_iota(jnp.int32, (1, bins), 1)
    bin_count = jnp.minimum(position + SMOOTH, bins - 1) - jnp.maximum(position - SMOOTH, 0) + 1
    inverse = 1.0 / bin_count.astype(jnp.float32)
    row = lax.broadcasted_iota(jnp.int32, (channels, 1), 0)
    live = jnp.zeros((channels, 1), jnp.float32)
    for channel in range(channels):
        live = jnp.where(row == channel, jnp.where(gap_ref[channel] == 0, 1.0, 0.0), live)
    pad = jnp.zeros((channels, TILE), jnp.float32)
    for window in range(windows):
        loads[window].wait()
        real_part = spectra[0, window].astype(jnp.float32)
        imag_part = spectra[1, window].astype(jnp.float32)
        magnitude = jnp.sqrt(real_part * real_part + imag_part * imag_part)
        band_mean = jnp.sum(magnitude, axis=1, keepdims=True) * (1.0 / bins)
        padded = jnp.concatenate([magnitude, pad], axis=1)
        width = bins + TILE
        total = padded
        for step in (1, 2, 4, 8):
            total = total + pltpu.roll(total, step, 1)
        near = pltpu.roll(total, width - SMOOTH, 1) + pltpu.roll(padded, SMOOTH, 1)
        divisor = near[:, :bins] * inverse + water_level * band_mean + 1e-06
        factor = live / divisor
        white_real = (real_part * factor).astype(jnp.bfloat16)
        white_imag = (imag_part * factor).astype(jnp.bfloat16)
        for tile in range(tiles):
            rows = slice(tile * channels, (tile + 1) * channels)
            lanes = slice(tile * TILE, (tile + 1) * TILE)
            held[rows, 2 * window * TILE : (2 * window + 1) * TILE] = white_real[:, lanes]
            held[rows, (2 * window + 1) * TILE : (2 * window + 2) * TILE] = white_imag[:, lanes]

    def ordered(source, store):
        first = jnp.dot(source[:, : 8 * TILE], main[...], preferred_element_type=jnp.float32).astype(jnp.bfloat16)
        last = jnp.dot(source[:, 8 * TILE :], rest[...], preferred_element_type=jnp.float32).astype(jnp.bfloat16)
        for tile in range(tiles):
            rows = slice(tile * channels, (tile + 1) * channels)
            for half in range(2):
                quad = tile * 2 + half
                chunk, start = quad // (CHUNK // QUAD), quad % (CHUNK // QUAD) * QUAD_LANES
                store(chunk, slice(start, start + 4 * TILE), first[rows, half * 4 * TILE : (half + 1) * 4 * TILE])
                store(
                    chunk, slice(start + 4 * TILE, start + QUAD_LANES), last[rows, half * TILE : (half + 1) * TILE]
                )

    def store_around(chunk, lanes, value):
        around[chunk, :channels, lanes] = value

    def store_turned(chunk, lanes, value):
        turned[chunk, :, lanes] = value

    loads[windows].wait()
    loads[windows + 1].wait()
    ordered(held[...], store_around)

    def halo(chunk, place):
        return pltpu.make_async_remote_copy(
            src_ref=around.at[chunk, pl.ds(0, channels), :],
            dst_ref=around.at[chunk, pl.ds((place + 1) * channels, channels), :],
            send_sem=halo_send.at[chunk, place],
            recv_sem=halo_recv.at[chunk, place],
            device_id={"chan": block(-OFFSETS[place]), "win": win},
            device_id_type=MESH,
        )

    pl.semaphore_wait(barrier, 2 * BLOCKS + 2)
    for chunk in range(chunks):
        for place in range(BLOCKS):
            halo(chunk, place).start()

    parts = held[...]
    swapped = [parts[:, (i ^ 1) * TILE : ((i ^ 1) + 1) * TILE] for i in range(2 * windows)]
    swapped = [-one if i % 2 else one for i, one in enumerate(swapped)]
    ordered(jnp.concatenate(swapped, axis=1), store_turned)
    even[...] = jnp.zeros_like(even)
    odd[...] = jnp.zeros_like(odd)
    lags[:, span + BLOCKS * channels :, :] = jnp.zeros((channels, channels, LAGS), jnp.bfloat16)

    loads[windows + 2].wait()
    loads[windows + 3].wait()
    lane = lax.broadcasted_iota(jnp.int32, (1, 2 * span), 1)
    column = lane
    for place, offset in enumerate(OFFSETS):
        column = jnp.where(lane // channels == place + 1, lane + (offset - place - 1) * channels, column)
        column = jnp.where(lane // channels == place + 1 + BLOCKS, lane - (offset + place + 1 + BLOCKS) * channels, column)
    column = jnp.where(lane // channels == 2 * BLOCKS + 1, 2**20, column).astype(jnp.float32)
    relative = jnp.where(mask[...] > 0, partners[...] - me * channels, -(2**20)).astype(jnp.float32)
    relative = jnp.concatenate([relative, jnp.zeros((TILE - channels, slots), jnp.float32)], axis=0).T
    for channel in range(channels):
        match = relative[:, channel : channel + 1] == column
        chosen[channel] = jnp.where(match, 1.0, 0.0).astype(jnp.bfloat16)

    row = lax.broadcasted_iota(jnp.int32, (SUB, TILE), 0)
    lane = lax.broadcasted_iota(jnp.int32, (SUB, TILE), 1)
    masks = []
    for group in range(QUAD // SUB):
        first = (lane % SUB == row).astype(jnp.float32)
        last = (lane % QUAD == group * SUB + row).astype(jnp.float32)
        masks.append(jnp.concatenate([first, last], axis=1).astype(jnp.bfloat16))
    loads[windows + 4].wait()
    loads[windows + 5].wait()

    def one_chunk(chunk, _):
        for place in range(BLOCKS):
            halo(chunk, place).wait_recv()

        def one_quad(quad, _):
            start = pl.multiple_of(quad * QUAD_LANES, TILE)

            def lane_tiles(ref, rows, group):
                first = ref[chunk, :rows, pl.ds(pl.multiple_of(start + group * TILE, TILE), TILE)]
                last = ref[chunk, :rows, pl.ds(pl.multiple_of(start + 4 * TILE, TILE), TILE)]
                return jnp.concatenate([first, last], axis=1)

            for group in range(QUAD // SUB):
                others = lane_tiles(around, span, group)
                for part, ref in ((0, around), (1, turned)):
                    own = lane_tiles(ref, channels, group)
                    spread = (own[:, None, :] * masks[group][None, :, :]).reshape(channels * SUB, 2 * TILE)
                    product = lax.dot_general(
                        spread, others, (((1,), (1,)), ((), ())), preferred_element_type=jnp.float32
                    )
                    first_bin = pl.multiple_of(quad * QUAD + group * SUB, SUB)
                    cross[part, :, pl.ds(first_bin, SUB), :] = product.astype(jnp.bfloat16).reshape(channels, SUB, span)
            return 0

        lax.fori_loop(0, CHUNK // QUAD, one_quad, 0)

        def some_channels(number, _):
            first = number * ABREAST
            for part, table, total in ((0, cos_table, even), (1, sin_table, odd)):
                rows = jnp.concatenate([cross[part, first + i].T for i in range(ABREAST)], axis=0)
                result = jnp.dot(rows, table[chunk], preferred_element_type=jnp.float32)
                total[pl.ds(first, ABREAST)] += result.reshape(ABREAST, span, LAGS)
            return 0

        lax.fori_loop(0, channels // ABREAST, some_channels, 0)
        return 0

    lax.fori_loop(0, chunks, one_chunk, 0)

    for channel in range(channels):
        cos_sum = even[channel]
        sin_sum = odd[channel]
        lags[channel, :span, :] = (cos_sum - sin_sum).astype(jnp.bfloat16)
        back_sum = (cos_sum + sin_sum)[channels:]
        for half in range(LAGS // TILE):
            lanes = slice(half * TILE, (half + 1) * TILE)
            mirrored[half, pl.ds(channel, BLOCKS * channels, stride=channels), :] = back_sum[:, lanes]

    def back(group, place):
        return pltpu.make_async_remote_copy(
            src_ref=back_out.at[group, place],
            dst_ref=lags.at[pl.ds(group * few, few), pl.ds(span + place * channels, channels), :],
            send_sem=back_send.at[group, place],
            recv_sem=back_recv.at[group, place],
            device_id={"chan": block(OFFSETS[place]), "win": win},
            device_id_type=MESH,
        )

    for group in range(GROUPS):
        for place in range(BLOCKS):
            first = (place * channels + group * few) * channels
            for half in range(LAGS // TILE):
                rows = mirrored[half, first : first + few * channels].astype(jnp.bfloat16)
                lanes = slice(half * TILE, (half + 1) * TILE)
                back_out[group, place, :, :, lanes] = rows.reshape(few, channels, TILE)
            back(group, place).start()

    def slots_of(owner):
        return pl.ds(pl.multiple_of(owner * share, share), share)

    def to_core(group, half):
        return pltpu.make_async_remote_copy(
            src_ref=picked.at[pl.ds(group * few, few), slots_of(2 * half + 1 - core), :],
            dst_ref=from_core.at[half, pl.ds(group * few, few)],
            send_sem=core_send.at[group, half],
            recv_sem=core_recv.at[group, half],
            device_id={"chan": me, "win": other_core},
            device_id_type=MESH,
        )

    def away(group):
        return pltpu.make_async_remote_copy(
            src_ref=to_far.at[pl.ds(group * few, few)],
            dst_ref=from_far.at[pl.ds(group * few, few)],
            send_sem=far_send.at[group],
            recv_sem=far_recv.at[group],
            device_id={"chan": me, "win": other_far},
            device_id_type=MESH,
        )

    for group in range(GROUPS + 1):
        if group < GROUPS:
            for place in range(BLOCKS):
                back(group, place).wait_recv()
            for channel in range(group * few, (group + 1) * few):
                rows = jnp.dot(chosen[channel], lags[channel], preferred_element_type=jnp.float32)
                picked[channel] = rows.astype(jnp.bfloat16)
            for half in range(2):
                to_core(group, half).start()
        if group > 0:
            for half in range(2):
                to_core(group - 1, half).wait_recv()
            for channel in range((group - 1) * few, group * few):
                mine = picked[channel, slots_of(other_far), :].astype(jnp.float32)
                theirs = from_core[1 - far, channel].astype(jnp.float32)
                to_far[channel] = (mine + theirs).astype(jnp.bfloat16)
            away(group - 1).start()
    scale = 1.0 / math.sqrt(windows * lax.axis_size("win") * bins)
    for group in range(GROUPS):
        away(group).wait_recv()
        for channel in range(group * few, (group + 1) * few):
            mine = picked[channel, slots_of(win), :].astype(jnp.float32)
            theirs = from_core[far, channel].astype(jnp.float32) + from_far[channel].astype(jnp.float32)
            for half in range(LAGS // TILE):
                lanes = slice(half * TILE, (half + 1) * TILE)
                out_ref[half, pl.ds(channel, share, stride=channels), :] = ((mine + theirs) * scale)[:, lanes]

    for chunk in range(chunks):
        for place in range(BLOCKS):
            halo(chunk, place).wait_send()
    for group in range(GROUPS):
        for place in range(BLOCKS):
            back(group, place).wait_send()
        for half in range(2):
            to_core(group, half).wait_send()
        away(group).wait_send()


def on_device(spectra, partners, pair_mask, gap_flags):
    _, windows, channels, bins = spectra.shape
    slots = partners.shape[1]
    chunks = bins // CHUNK
    span = (BLOCKS + 1) * channels
    share = slots // 4
    bf16 = jnp.bfloat16
    main, rest = bin_order()
    cos_table, sin_table = lag_tables(bins)
    anywhere = pl.BlockSpec(memory_space=pl.ANY)
    scalars = pl.BlockSpec(memory_space=pltpu.SMEM)
    semaphores = pltpu.SemaphoreType.DMA
    stacked = pl.pallas_call(
        kernel,
        out_shape=jax.ShapeDtypeStruct((LAGS // TILE, share * channels, TILE), jnp.float32),
        in_specs=[anywhere] * 3 + [scalars] + [anywhere] * 4,
        out_specs=pl.BlockSpec(memory_space=pltpu.VMEM),
        scratch_shapes=[
            pltpu.VMEM(spectra.shape, bf16),
            pltpu.VMEM(partners.shape, jnp.int32),
            pltpu.VMEM(pair_mask.shape, jnp.int32),
            pltpu.VMEM(main.shape, bf16),
            pltpu.VMEM(rest.shape, bf16),
            pltpu.VMEM(cos_table.shape, bf16),
            pltpu.VMEM(sin_table.shape, bf16),
            pltpu.VMEM((bins // TILE * channels, 2 * windows * TILE), bf16),
            pltpu.VMEM((chunks, channels, CHUNK_LANES), bf16),
            pltpu.VMEM((chunks, span, CHUNK_LANES), bf16),
            pltpu.VMEM((2, channels, CHUNK, span), bf16),
            pltpu.VMEM((channels, span, LAGS), jnp.float32),
            pltpu.VMEM((channels, span, LAGS), jnp.float32),
            pltpu.VMEM((channels, slots, 2 * span), bf16),
            pltpu.VMEM((LAGS // TILE, BLOCKS * channels * channels, TILE), jnp.float32),
            pltpu.VMEM((channels, 2 * span, LAGS), bf16),
            pltpu.VMEM((GROUPS, BLOCKS, channels // GROUPS, channels, LAGS), bf16),
            pltpu.VMEM((channels, slots, LAGS), bf16),
            pltpu.VMEM((2, channels, share, LAGS), bf16),
            pltpu.VMEM((channels, share, LAGS), bf16),
            pltpu.VMEM((channels, share, LAGS), bf16),
            semaphores((windows + 6,)),
            semaphores((chunks, BLOCKS)),
            semaphores((chunks, BLOCKS)),
            semaphores((GROUPS, BLOCKS)),
            semaphores((GROUPS, BLOCKS)),
            semaphores((GROUPS, 2)),
            semaphores((GROUPS, 2)),
            semaphores((GROUPS,)),
            semaphores((GROUPS,)),
        ],
        compiler_params=pltpu.CompilerParams(
            collective_id=0, has_side_effects=True, vmem_limit_bytes=56 * 2**20
        ),
        name="stack",
    )(spectra, partners, pair_mask, gap_flags, main, rest, cos_table, sin_table)
    stacked = stacked.reshape(LAGS // TILE, share, channels, TILE)
    return jnp.transpose(stacked, (1, 2, 0, 3)).reshape(share, channels, LAGS)


def solution(mesh):
    placed = (P(None, "win", "chan", None), P("chan", None), P("chan", None), P("chan"))
    return jax.shard_map(
        on_device, mesh=mesh, in_specs=placed, out_specs=P("win", "chan", None), check_vma=False
    )
```

```python
import math

import jax
import jax.numpy as jnp
import numpy as np
from jax import lax
from jax.experimental import pallas as pl
from jax.experimental.pallas import tpu as pltpu
from jax.sharding import PartitionSpec as P

LAGS = 256
SMOOTH = 8
FLO = 64
NSAMP = 6000
water_level = 0.1

MESH = pl.DeviceIdType.MESH
OFFSETS = (1, -2, 3, 4, -5, -6, 7)
BLOCKS = len(OFFSETS)
FIRST, SECOND = 1, 5
RELAY = OFFSETS[SECOND] - OFFSETS[FIRST]
LAST = BLOCKS - 1
EDGE = 4
TILE = 128
SUB = 16
QUAD = 64
QUAD_LANES = 640
CHUNK = 256
CHUNK_LANES = CHUNK // QUAD * QUAD_LANES
GROUPS = 8
ABREAST = 4


def bin_order():
    main = np.zeros((8 * TILE, 8 * TILE), np.float32)
    part, f = np.meshgrid(np.arange(8), np.arange(TILE), indexing="ij")
    main[part * TILE + f, (f // SUB) * TILE + part * SUB + f % SUB] = 1.0
    rest = np.zeros((2 * TILE, 2 * TILE), np.float32)
    part, f = np.meshgrid(np.arange(2), np.arange(TILE), indexing="ij")
    rest[part * TILE + f, (f // QUAD) * TILE + part * QUAD + f % QUAD] = 1.0
    return main.astype(jnp.bfloat16), rest.astype(jnp.bfloat16)


def lag_tables(bins):
    steps = np.mod((FLO + np.arange(bins))[:, None] * (np.arange(LAGS) - LAGS // 2)[None, :], NSAMP)
    angles = steps.astype(np.float64) * (2.0 * math.pi / NSAMP)
    shape = (bins // CHUNK, CHUNK, LAGS)
    return (
        np.cos(angles).astype(np.float32).reshape(shape).astype(jnp.bfloat16),
        np.sin(angles).astype(np.float32).reshape(shape).astype(jnp.bfloat16),
    )


def kernel(
    spectra_ref, partners_ref, mask_ref, gap_ref, main_ref, rest_ref, cos_ref, sin_ref, out_ref,
    spectra, partners, mask, main, rest, cos_table, sin_table,
    held, turned, around, edge_out, edge_in, cross, even, odd, chosen, mirrored, lags, back_out, picked, from_core, to_far, from_far,
    load_sem, halo_send, halo_recv, back_send, back_recv, core_send, core_recv, far_send, far_recv,
):
    windows, channels, bins = spectra.shape[1:]
    tiles = bins // TILE
    chunks = bins // CHUNK
    span = around.shape[1]
    slots = partners.shape[1]
    share = slots // 4
    few = channels // GROUPS
    count = lax.axis_size("chan")
    me = lax.axis_index("chan")
    win = lax.axis_index("win")
    core = lax.rem(win, 2)
    far = win // 2
    other_core = win + 1 - 2 * core
    other_far = lax.rem(win + 2, 4)

    def block(offset):
        return lax.rem(me + count + offset, count)

    loads = [(spectra_ref.at[:, window], spectra.at[:, window]) for window in range(windows)]
    loads += [(main_ref, main), (rest_ref, rest), (partners_ref, partners), (mask_ref, mask)]
    loads += [(cos_ref, cos_table), (sin_ref, sin_table)]
    loads = [pltpu.make_async_copy(source, target, load_sem.at[i]) for i, (source, target) in enumerate(loads)]
    for load in loads:
        load.start()
    barrier = pltpu.get_barrier_semaphore()
    for offset in OFFSETS:
        for chan in (block(offset), block(-offset)):
            pl.semaphore_signal(barrier, inc=1, device_id={"chan": chan, "win": win}, device_id_type=MESH)
    for partner in (other_core, other_far):
        pl.semaphore_signal(barrier, inc=1, device_id={"chan": me, "win": partner}, device_id_type=MESH)

    position = lax.broadcasted_iota(jnp.int32, (1, bins), 1)
    bin_count = jnp.minimum(position + SMOOTH, bins - 1) - jnp.maximum(position - SMOOTH, 0) + 1
    inverse = 1.0 / bin_count.astype(jnp.float32)
    row = lax.broadcasted_iota(jnp.int32, (channels, 1), 0)
    live = jnp.zeros((channels, 1), jnp.float32)
    for channel in range(channels):
        live = jnp.where(row == channel, jnp.where(gap_ref[channel] == 0, 1.0, 0.0), live)
    pad = jnp.zeros((channels, TILE), jnp.float32)
    for window in range(windows):
        loads[window].wait()
        real_part = spectra[0, window].astype(jnp.float32)
        imag_part = spectra[1, window].astype(jnp.float32)
        magnitude = jnp.sqrt(real_part * real_part + imag_part * imag_part)
        band_mean = jnp.sum(magnitude, axis=1, keepdims=True) * (1.0 / bins)
        padded = jnp.concatenate([magnitude, pad], axis=1)
        width = bins + TILE
        total = padded
        for step in (1, 2, 4, 8):
            total = total + pltpu.roll(total, step, 1)
        near = pltpu.roll(total, width - SMOOTH, 1) + pltpu.roll(padded, SMOOTH, 1)
        divisor = near[:, :bins] * inverse + water_level * band_mean + 1e-06
        factor = live / divisor
        white_real = (real_part * factor).astype(jnp.bfloat16)
        white_imag = (imag_part * factor).astype(jnp.bfloat16)
        for tile in range(tiles):
            rows = slice(tile * channels, (tile + 1) * channels)
            lanes = slice(tile * TILE, (tile + 1) * TILE)
            held[rows, 2 * window * TILE : (2 * window + 1) * TILE] = white_real[:, lanes]
            held[rows, (2 * window + 1) * TILE : (2 * window + 2) * TILE] = white_imag[:, lanes]

    def ordered(source, store):
        wide_first = jnp.dot(source[:, : 8 * TILE], main[...], preferred_element_type=jnp.float32)
        wide_last = jnp.dot(source[:, 8 * TILE :], rest[...], preferred_element_type=jnp.float32)
        first, last = wide_first.astype(jnp.bfloat16), wide_last.astype(jnp.bfloat16)
        for tile in range(tiles):
            rows = slice(tile * channels, (tile + 1) * channels)
            for half in range(2):
                quad = tile * 2 + half
                chunk, start = quad // (CHUNK // QUAD), quad % (CHUNK // QUAD) * QUAD_LANES
                store(chunk, slice(start, start + 4 * TILE), first[rows, half * 4 * TILE : (half + 1) * 4 * TILE])
                store(
                    chunk, slice(start + 4 * TILE, start + QUAD_LANES), last[rows, half * TILE : (half + 1) * TILE]
                )
        return wide_first, wide_last

    def store_around(chunk, lanes, value):
        around[chunk, :channels, lanes] = value

    def store_turned(chunk, lanes, value):
        turned[chunk, :, lanes] = value

    loads[windows].wait()
    loads[windows + 1].wait()
    wide_first, wide_last = ordered(held[...], store_around)
    for chunk in range(chunks):
        pieces = []
        for quad in range(CHUNK // QUAD):
            tile, half = divmod(chunk * (CHUNK // QUAD) + quad, 2)
            rows = slice(tile * channels, tile * channels + EDGE)
            first = wide_first[rows, half * 4 * TILE : (half + 1) * 4 * TILE]
            last = wide_last[rows, half * TILE : (half + 1) * TILE]
            pieces.append(jnp.concatenate([first, last], axis=1))
        edge_out[chunk] = jnp.concatenate(pieces, axis=0).astype(jnp.bfloat16)

    def halo(chunk, place):
        if place == LAST:
            source, target = edge_out.at[chunk], edge_in.at[chunk]
        else:
            first = (FIRST + 1) * channels if place == SECOND else 0
            source = around.at[chunk, pl.ds(first, channels), :]
            target = around.at[chunk, pl.ds((place + 1) * channels, channels), :]
        return pltpu.make_async_remote_copy(
            src_ref=source,
            dst_ref=target,
            send_sem=halo_send.at[chunk, place],
            recv_sem=halo_recv.at[chunk, place],
            device_id={"chan": block(-RELAY if place == SECOND else -OFFSETS[place]), "win": win},
            device_id_type=MESH,
        )

    pl.semaphore_wait(barrier, 2 * BLOCKS + 2)
    halo(0, FIRST).start()
    halo(1, FIRST).start()
    for chunk in range(chunks):
        for place in range(BLOCKS):
            if place not in (FIRST, SECOND):
                halo(chunk, place).start()
        if chunk + 2 < chunks:
            halo(chunk + 2, FIRST).start()

    parts = held[...]
    swapped = [parts[:, (i ^ 1) * TILE : ((i ^ 1) + 1) * TILE] for i in range(2 * windows)]
    swapped = [-one if i % 2 else one for i, one in enumerate(swapped)]
    ordered(jnp.concatenate(swapped, axis=1), store_turned)
    even[...] = jnp.zeros_like(even)
    odd[...] = jnp.zeros_like(odd)
    lags[:, span + BLOCKS * channels :, :] = jnp.zeros((channels, channels, LAGS), jnp.bfloat16)
    lags[EDGE:, span + LAST * channels : span + BLOCKS * channels, :] = jnp.zeros(
        (channels - EDGE, channels, LAGS), jnp.bfloat16
    )

    loads[windows + 2].wait()
    loads[windows + 3].wait()
    lane = lax.broadcasted_iota(jnp.int32, (1, 2 * span), 1)
    column = lane
    for place, offset in enumerate(OFFSETS):
        column = jnp.where(lane // channels == place + 1, lane + (offset - place - 1) * channels, column)
        column = jnp.where(lane // channels == place + 1 + BLOCKS, lane - (offset + place + 1 + BLOCKS) * channels, column)
    column = jnp.where(lane // channels == 2 * BLOCKS + 1, 2**20, column).astype(jnp.float32)
    relative = jnp.where(mask[...] > 0, partners[...] - me * channels, -(2**20)).astype(jnp.float32)
    relative = jnp.concatenate([relative, jnp.zeros((TILE - channels, slots), jnp.float32)], axis=0).T
    for channel in range(channels):
        match = relative[:, channel : channel + 1] == column
        chosen[channel] = jnp.where(match, 1.0, 0.0).astype(jnp.bfloat16)

    row = lax.broadcasted_iota(jnp.int32, (SUB, TILE), 0)
    lane = lax.broadcasted_iota(jnp.int32, (SUB, TILE), 1)
    masks = []
    for group in range(QUAD // SUB):
        first = (lane % SUB == row).astype(jnp.float32)
        last = (lane % QUAD == group * SUB + row).astype(jnp.float32)
        masks.append(jnp.concatenate([first, last], axis=1).astype(jnp.bfloat16))
    loads[windows + 4].wait()
    loads[windows + 5].wait()

    def relay(chunk):
        halo(chunk, FIRST).wait_recv()
        halo(chunk, SECOND).start()

    relay(0)

    def one_chunk(chunk, _):
        @pl.when(chunk + 1 < chunks)
        def _():
            relay(chunk + 1)

        for place in range(BLOCKS):
            if place != FIRST:
                halo(chunk, place).wait_recv()
        edge = edge_in[chunk].astype(jnp.float32)
        for quad in range(CHUNK // QUAD):
            shift = (channels - quad * EDGE) % channels
            rows = (pltpu.roll(edge, shift, 0) if shift else edge).astype(jnp.bfloat16)
            around[chunk, span - channels :, quad * QUAD_LANES : (quad + 1) * QUAD_LANES] = rows

        def one_quad(quad, _):
            start = pl.multiple_of(quad * QUAD_LANES, TILE)

            def lane_tiles(ref, rows, group):
                first = ref[chunk, :rows, pl.ds(pl.multiple_of(start + group * TILE, TILE), TILE)]
                last = ref[chunk, :rows, pl.ds(pl.multiple_of(start + 4 * TILE, TILE), TILE)]
                return jnp.concatenate([first, last], axis=1)

            for group in range(QUAD // SUB):
                others = lane_tiles(around, span, group)
                for part, ref in ((0, around), (1, turned)):
                    own = lane_tiles(ref, channels, group)
                    spread = (own[:, None, :] * masks[group][None, :, :]).reshape(channels * SUB, 2 * TILE)
                    product = lax.dot_general(
                        spread, others, (((1,), (1,)), ((), ())), preferred_element_type=jnp.float32
                    )
                    first_bin = pl.multiple_of(quad * QUAD + group * SUB, SUB)
                    cross[part, :, pl.ds(first_bin, SUB), :] = product.astype(jnp.bfloat16).reshape(channels, SUB, span)
            return 0

        lax.fori_loop(0, CHUNK // QUAD, one_quad, 0)

        def some_channels(number, _):
            first = number * ABREAST
            for part, table, total in ((0, cos_table, even), (1, sin_table, odd)):
                rows = jnp.concatenate([cross[part, first + i].T for i in range(ABREAST)], axis=0)
                result = jnp.dot(rows, table[chunk], preferred_element_type=jnp.float32)
                total[pl.ds(first, ABREAST)] += result.reshape(ABREAST, span, LAGS)
            return 0

        lax.fori_loop(0, channels // ABREAST, some_channels, 0)
        return 0

    lax.fori_loop(0, chunks, one_chunk, 0)

    for channel in range(channels):
        cos_sum = even[channel]
        sin_sum = odd[channel]
        lags[channel, :span, :] = (cos_sum - sin_sum).astype(jnp.bfloat16)
        back_sum = (cos_sum + sin_sum)[channels:]
        for half in range(LAGS // TILE):
            lanes = slice(half * TILE, (half + 1) * TILE)
            mirrored[half, pl.ds(channel, BLOCKS * channels, stride=channels), :] = back_sum[:, lanes]

    def travels(group, place):
        return place != LAST or group * few < EDGE

    def back(group, place):
        return pltpu.make_async_remote_copy(
            src_ref=back_out.at[group, place],
            dst_ref=lags.at[pl.ds(group * few, few), pl.ds(span + place * channels, channels), :],
            send_sem=back_send.at[group, place],
            recv_sem=back_recv.at[group, place],
            device_id={"chan": block(OFFSETS[place]), "win": win},
            device_id_type=MESH,
        )

    for group in range(GROUPS):
        for place in range(BLOCKS):
            if not travels(group, place):
                continue
            first = (place * channels + group * few) * channels
            for half in range(LAGS // TILE):
                rows = mirrored[half, first : first + few * channels].astype(jnp.bfloat16)
                lanes = slice(half * TILE, (half + 1) * TILE)
                back_out[group, place, :, :, lanes] = rows.reshape(few, channels, TILE)
            back(group, place).start()

    def slots_of(owner):
        return pl.ds(pl.multiple_of(owner * share, share), share)

    def to_core(group, half):
        return pltpu.make_async_remote_copy(
            src_ref=picked.at[pl.ds(group * few, few), slots_of(2 * half + 1 - core), :],
            dst_ref=from_core.at[half, pl.ds(group * few, few)],
            send_sem=core_send.at[group, half],
            recv_sem=core_recv.at[group, half],
            device_id={"chan": me, "win": other_core},
            device_id_type=MESH,
        )

    def away(group):
        return pltpu.make_async_remote_copy(
            src_ref=to_far.at[pl.ds(group * few, few)],
            dst_ref=from_far.at[pl.ds(group * few, few)],
            send_sem=far_send.at[group],
            recv_sem=far_recv.at[group],
            device_id={"chan": me, "win": other_far},
            device_id_type=MESH,
        )

    for group in range(GROUPS + 1):
        if group < GROUPS:
            for place in range(BLOCKS):
                if travels(group, place):
                    back(group, place).wait_recv()
            for channel in range(group * few, (group + 1) * few):
                rows = jnp.dot(chosen[channel], lags[channel], preferred_element_type=jnp.float32)
                picked[channel] = rows.astype(jnp.bfloat16)
            for half in range(2):
                to_core(group, half).start()
        if group > 0:
            for half in range(2):
                to_core(group - 1, half).wait_recv()
            for channel in range((group - 1) * few, group * few):
                mine = picked[channel, slots_of(other_far), :].astype(jnp.float32)
                theirs = from_core[1 - far, channel].astype(jnp.float32)
                to_far[channel] = (mine + theirs).astype(jnp.bfloat16)
            away(group - 1).start()
    scale = 1.0 / math.sqrt(windows * lax.axis_size("win") * bins)
    for group in range(GROUPS):
        away(group).wait_recv()
        for channel in range(group * few, (group + 1) * few):
            mine = picked[channel, slots_of(win), :].astype(jnp.float32)
            theirs = from_core[far, channel].astype(jnp.float32) + from_far[channel].astype(jnp.float32)
            for half in range(LAGS // TILE):
                lanes = slice(half * TILE, (half + 1) * TILE)
                out_ref[half, pl.ds(channel, share, stride=channels), :] = ((mine + theirs) * scale)[:, lanes]

    for chunk in range(chunks):
        for place in range(BLOCKS):
            halo(chunk, place).wait_send()
    for group in range(GROUPS):
        for place in range(BLOCKS):
            if travels(group, place):
                back(group, place).wait_send()
        for half in range(2):
            to_core(group, half).wait_send()
        away(group).wait_send()


def on_device(spectra, partners, pair_mask, gap_flags):
    _, windows, channels, bins = spectra.shape
    slots = partners.shape[1]
    chunks = bins // CHUNK
    span = (BLOCKS + 1) * channels
    share = slots // 4
    bf16 = jnp.bfloat16
    main, rest = bin_order()
    cos_table, sin_table = lag_tables(bins)
    anywhere = pl.BlockSpec(memory_space=pl.ANY)
    scalars = pl.BlockSpec(memory_space=pltpu.SMEM)
    semaphores = pltpu.SemaphoreType.DMA
    stacked = pl.pallas_call(
        kernel,
        out_shape=jax.ShapeDtypeStruct((LAGS // TILE, share * channels, TILE), jnp.float32),
        in_specs=[anywhere] * 3 + [scalars] + [anywhere] * 4,
        out_specs=pl.BlockSpec(memory_space=pltpu.VMEM),
        scratch_shapes=[
            pltpu.VMEM(spectra.shape, bf16),
            pltpu.VMEM(partners.shape, jnp.int32),
            pltpu.VMEM(pair_mask.shape, jnp.int32),
            pltpu.VMEM(main.shape, bf16),
            pltpu.VMEM(rest.shape, bf16),
            pltpu.VMEM(cos_table.shape, bf16),
            pltpu.VMEM(sin_table.shape, bf16),
            pltpu.VMEM((bins // TILE * channels, 2 * windows * TILE), bf16),
            pltpu.VMEM((chunks, channels, CHUNK_LANES), bf16),
            pltpu.VMEM((chunks, span, CHUNK_LANES), bf16),
            pltpu.VMEM((chunks, channels, QUAD_LANES), bf16),
            pltpu.VMEM((chunks, channels, QUAD_LANES), bf16),
            pltpu.VMEM((2, channels, CHUNK, span), bf16),
            pltpu.VMEM((channels, span, LAGS), jnp.float32),
            pltpu.VMEM((channels, span, LAGS), jnp.float32),
            pltpu.VMEM((channels, slots, 2 * span), bf16),
            pltpu.VMEM((LAGS // TILE, BLOCKS * channels * channels, TILE), jnp.float32),
            pltpu.VMEM((channels, 2 * span, LAGS), bf16),
            pltpu.VMEM((GROUPS, BLOCKS, channels // GROUPS, channels, LAGS), bf16),
            pltpu.VMEM((channels, slots, LAGS), bf16),
            pltpu.VMEM((2, channels, share, LAGS), bf16),
            pltpu.VMEM((channels, share, LAGS), bf16),
            pltpu.VMEM((channels, share, LAGS), bf16),
            semaphores((windows + 6,)),
            semaphores((chunks, BLOCKS)),
            semaphores((chunks, BLOCKS)),
            semaphores((GROUPS, BLOCKS)),
            semaphores((GROUPS, BLOCKS)),
            semaphores((GROUPS, 2)),
            semaphores((GROUPS, 2)),
            semaphores((GROUPS,)),
            semaphores((GROUPS,)),
        ],
        compiler_params=pltpu.CompilerParams(
            collective_id=0, has_side_effects=True, vmem_limit_bytes=56 * 2**20
        ),
        name="stack",
    )(spectra, partners, pair_mask, gap_flags, main, rest, cos_table, sin_table)
    stacked = stacked.reshape(LAGS // TILE, share, channels, TILE)
    return jnp.transpose(stacked, (1, 2, 0, 3)).reshape(share, channels, LAGS)


def solution(mesh):
    placed = (P(None, "win", "chan", None), P("chan", None), P("chan", None), P("chan"))
    return jax.shard_map(
        on_device, mesh=mesh, in_specs=placed, out_specs=P("win", "chan", None), check_vma=False
    )
```

```python
import math

import jax
import jax.numpy as jnp
import numpy as np
from jax import lax
from jax.experimental import pallas as pl
from jax.experimental.pallas import tpu as pltpu
from jax.sharding import PartitionSpec as P

LAGS = 256
SMOOTH = 8
FLO = 64
NSAMP = 6000
water_level = 0.1

MESH = pl.DeviceIdType.MESH
OFFSETS = (1, -2, 3, 4, -5, -6, 7)
BLOCKS = len(OFFSETS)
FIRST, SECOND = 1, 5
RELAY = OFFSETS[SECOND] - OFFSETS[FIRST]
LAST = BLOCKS - 1
EDGE = 4
TILE = 128
SUB = 16
QUAD = 64
QUAD_LANES = 640
CHUNK = 256
CHUNK_LANES = CHUNK // QUAD * QUAD_LANES
RELAYED = 2
WINDOW = 2
GROUPS = 8
ABREAST = 16


def bin_order():
    main = np.zeros((8 * TILE, 8 * TILE), np.float32)
    part, f = np.meshgrid(np.arange(8), np.arange(TILE), indexing="ij")
    main[part * TILE + f, (f // SUB) * TILE + part * SUB + f % SUB] = 1.0
    rest = np.zeros((2 * TILE, 2 * TILE), np.float32)
    part, f = np.meshgrid(np.arange(2), np.arange(TILE), indexing="ij")
    rest[part * TILE + f, (f // QUAD) * TILE + part * QUAD + f % QUAD] = 1.0
    return main.astype(jnp.bfloat16), rest.astype(jnp.bfloat16)


def lag_tables(bins):
    steps = np.mod((FLO + np.arange(bins))[:, None] * (np.arange(LAGS) - LAGS // 2)[None, :], NSAMP)
    angles = steps.astype(np.float64) * (2.0 * math.pi / NSAMP)
    shape = (bins // CHUNK, CHUNK, LAGS)
    return (
        np.cos(angles).astype(np.float32).reshape(shape).astype(jnp.bfloat16),
        np.sin(angles).astype(np.float32).reshape(shape).astype(jnp.bfloat16),
    )


def kernel(
    spectra_ref, partners_ref, mask_ref, gap_ref, main_ref, rest_ref, cos_ref, sin_ref, out_ref,
    spectra, partners, mask, main, rest, cos_table, sin_table,
    held, turned, around, edge_out, edge_in, cross, even, odd, chosen, mirrored, lags, back_out, picked, from_core, to_far, from_far,
    load_sem, halo_send, halo_recv, back_send, back_recv, core_send, core_recv, far_send, far_recv,
):
    windows, channels, bins = spectra.shape[1:]
    tiles = bins // TILE
    chunks = bins // CHUNK
    span = around.shape[1]
    slots = partners.shape[1]
    share = slots // 4
    few = channels // GROUPS
    count = lax.axis_size("chan")
    me = lax.axis_index("chan")
    win = lax.axis_index("win")
    core = lax.rem(win, 2)
    far = win // 2
    other_core = win + 1 - 2 * core
    other_far = lax.rem(win + 2, 4)

    side = 1 - 2 * core

    def offset_of(place):
        return OFFSETS[place] if place == LAST else side * OFFSETS[place]

    def block(offset):
        return lax.rem(me + count + offset, count)

    loads = [(spectra_ref.at[:, window], spectra.at[:, window]) for window in range(windows)]
    loads += [(main_ref, main), (rest_ref, rest), (partners_ref, partners), (mask_ref, mask)]
    loads += [(cos_ref, cos_table), (sin_ref, sin_table)]
    loads = [pltpu.make_async_copy(source, target, load_sem.at[i]) for i, (source, target) in enumerate(loads)]
    for load in loads:
        load.start()
    barrier = pltpu.get_barrier_semaphore()
    for place in range(BLOCKS):
        for chan in (block(offset_of(place)), block(-offset_of(place))):
            pl.semaphore_signal(barrier, inc=1, device_id={"chan": chan, "win": win}, device_id_type=MESH)
    for partner in (other_core, other_far):
        pl.semaphore_signal(barrier, inc=1, device_id={"chan": me, "win": partner}, device_id_type=MESH)

    position = lax.broadcasted_iota(jnp.int32, (1, bins), 1)
    bin_count = jnp.minimum(position + SMOOTH, bins - 1) - jnp.maximum(position - SMOOTH, 0) + 1
    inverse = 1.0 / bin_count.astype(jnp.float32)
    row = lax.broadcasted_iota(jnp.int32, (channels, 1), 0)
    live = jnp.zeros((channels, 1), jnp.float32)
    for channel in range(channels):
        live = jnp.where(row == channel, jnp.where(gap_ref[channel] == 0, 1.0, 0.0), live)
    pad = jnp.zeros((channels, TILE), jnp.float32)
    for window in range(windows):
        loads[window].wait()
        real_part = spectra[0, window].astype(jnp.float32)
        imag_part = spectra[1, window].astype(jnp.float32)
        magnitude = jnp.sqrt(real_part * real_part + imag_part * imag_part)
        band_mean = jnp.sum(magnitude, axis=1, keepdims=True) * (1.0 / bins)
        padded = jnp.concatenate([magnitude, pad], axis=1)
        width = bins + TILE
        total = padded
        for step in (1, 2, 4, 8):
            total = total + pltpu.roll(total, step, 1)
        near = pltpu.roll(total, width - SMOOTH, 1) + pltpu.roll(padded, SMOOTH, 1)
        divisor = near[:, :bins] * inverse + water_level * band_mean + 1e-06
        factor = live / divisor
        white_real = (real_part * factor).astype(jnp.bfloat16)
        white_imag = (imag_part * factor).astype(jnp.bfloat16)
        for tile in range(tiles):
            rows = slice(tile * channels, (tile + 1) * channels)
            lanes = slice(tile * TILE, (tile + 1) * TILE)
            held[rows, 2 * window * TILE : (2 * window + 1) * TILE] = white_real[:, lanes]
            held[rows, (2 * window + 1) * TILE : (2 * window + 2) * TILE] = white_imag[:, lanes]

    def ordered(source, store):
        wide_first = jnp.dot(source[:, : 8 * TILE], main[...], preferred_element_type=jnp.float32)
        wide_last = jnp.dot(source[:, 8 * TILE :], rest[...], preferred_element_type=jnp.float32)
        first, last = wide_first.astype(jnp.bfloat16), wide_last.astype(jnp.bfloat16)
        for tile in range(tiles):
            rows = slice(tile * channels, (tile + 1) * channels)
            for half in range(2):
                quad = tile * 2 + half
                chunk, start = quad // (CHUNK // QUAD), quad % (CHUNK // QUAD) * QUAD_LANES
                store(chunk, slice(start, start + 4 * TILE), first[rows, half * 4 * TILE : (half + 1) * 4 * TILE])
                store(
                    chunk, slice(start + 4 * TILE, start + QUAD_LANES), last[rows, half * TILE : (half + 1) * TILE]
                )
        return wide_first, wide_last

    def store_around(chunk, lanes, value):
        around[chunk, :channels, lanes] = value

    def store_turned(chunk, lanes, value):
        turned[chunk, :, lanes] = value

    loads[windows].wait()
    loads[windows + 1].wait()
    wide_first, wide_last = ordered(held[...], store_around)
    for chunk in range(chunks):
        pieces = []
        for quad in range(CHUNK // QUAD):
            tile, half = divmod(chunk * (CHUNK // QUAD) + quad, 2)
            rows = slice(tile * channels, tile * channels + EDGE)
            first = wide_first[rows, half * 4 * TILE : (half + 1) * 4 * TILE]
            last = wide_last[rows, half * TILE : (half + 1) * TILE]
            pieces.append(jnp.concatenate([first, last], axis=1))
        edge_out[chunk] = jnp.concatenate(pieces, axis=0).astype(jnp.bfloat16)

    def halo(chunk, place):
        if place == LAST:
            source, target = edge_out.at[chunk], edge_in.at[chunk]
        else:
            first = (FIRST + 1) * channels if place == SECOND else 0
            source = around.at[chunk, pl.ds(first, channels), :]
            target = around.at[chunk, pl.ds((place + 1) * channels, channels), :]
        return pltpu.make_async_remote_copy(
            src_ref=source,
            dst_ref=target,
            send_sem=halo_send.at[chunk, place],
            recv_sem=halo_recv.at[chunk, place],
            device_id={"chan": block(-side * RELAY if place == SECOND else -offset_of(place)), "win": win},
            device_id_type=MESH,
        )

    pl.semaphore_wait(barrier, 2 * BLOCKS + 2)
    def send(chunk):
        for place in range(BLOCKS):
            if place not in (FIRST, SECOND):
                halo(chunk, place).start()

    for chunk in range(chunks):
        halo(chunk, FIRST).start()
    for chunk in range(min(WINDOW, chunks)):
        send(chunk)

    parts = held[...]
    swapped = [parts[:, (i ^ 1) * TILE : ((i ^ 1) + 1) * TILE] for i in range(2 * windows)]
    swapped = [-one if i % 2 else one for i, one in enumerate(swapped)]
    ordered(jnp.concatenate(swapped, axis=1), store_turned)
    even[...] = jnp.zeros_like(even)
    odd[...] = jnp.zeros_like(odd)
    lags[:, span + BLOCKS * channels :, :] = jnp.zeros((channels, channels, LAGS), jnp.bfloat16)
    lags[EDGE:, span + LAST * channels : span + BLOCKS * channels, :] = jnp.zeros(
        (channels - EDGE, channels, LAGS), jnp.bfloat16
    )

    loads[windows + 2].wait()
    loads[windows + 3].wait()
    lane = lax.broadcasted_iota(jnp.int32, (1, 2 * span), 1)
    column = lane
    for place in range(BLOCKS):
        offset = offset_of(place)
        column = jnp.where(lane // channels == place + 1, lane + (offset - place - 1) * channels, column)
        column = jnp.where(lane // channels == place + 1 + BLOCKS, lane - (offset + place + 1 + BLOCKS) * channels, column)
    column = jnp.where(lane // channels == 2 * BLOCKS + 1, 2**20, column).astype(jnp.float32)
    relative = jnp.where(mask[...] > 0, partners[...] - me * channels, -(2**20)).astype(jnp.float32)
    relative = jnp.concatenate([relative, jnp.zeros((TILE - channels, slots), jnp.float32)], axis=0).T
    for channel in range(channels):
        match = relative[:, channel : channel + 1] == column
        chosen[channel] = jnp.where(match, 1.0, 0.0).astype(jnp.bfloat16)

    row = lax.broadcasted_iota(jnp.int32, (SUB, TILE), 0)
    lane = lax.broadcasted_iota(jnp.int32, (SUB, TILE), 1)
    masks = []
    for group in range(QUAD // SUB):
        first = (lane % SUB == row).astype(jnp.float32)
        last = (lane % QUAD == group * SUB + row).astype(jnp.float32)
        masks.append(jnp.concatenate([first, last], axis=1).astype(jnp.bfloat16))
    loads[windows + 4].wait()
    loads[windows + 5].wait()

    def relay(chunk):
        halo(chunk, FIRST).wait_recv()
        halo(chunk, SECOND).start()

    for chunk in range(min(RELAYED, chunks)):
        relay(chunk)

    def one_chunk(chunk, _):
        @pl.when(chunk + RELAYED < chunks)
        def _():
            relay(chunk + RELAYED)

        @pl.when(chunk + WINDOW < chunks)
        def _():
            send(chunk + WINDOW)

        for place in range(BLOCKS):
            if place != FIRST:
                halo(chunk, place).wait_recv()
        edge = edge_in[chunk].astype(jnp.float32)
        for quad in range(CHUNK // QUAD):
            shift = (channels - quad * EDGE) % channels
            rows = (pltpu.roll(edge, shift, 0) if shift else edge).astype(jnp.bfloat16)
            around[chunk, span - channels :, quad * QUAD_LANES : (quad + 1) * QUAD_LANES] = rows

        def one_quad(quad, _):
            start = pl.multiple_of(quad * QUAD_LANES, TILE)

            def lane_tiles(ref, rows, group):
                first = ref[chunk, :rows, pl.ds(pl.multiple_of(start + group * TILE, TILE), TILE)]
                last = ref[chunk, :rows, pl.ds(pl.multiple_of(start + 4 * TILE, TILE), TILE)]
                return jnp.concatenate([first, last], axis=1)

            for group in range(QUAD // SUB):
                others = lane_tiles(around, span, group)
                own = jnp.concatenate([lane_tiles(ref, channels, group) for ref in (around, turned)], axis=0)
                spread = (own[:, None, :] * masks[group][None, :, :]).reshape(2 * channels * SUB, 2 * TILE)
                product = lax.dot_general(
                    spread, others, (((1,), (1,)), ((), ())), preferred_element_type=jnp.float32
                )
                first_bin = pl.multiple_of(quad * QUAD + group * SUB, SUB)
                product = product.astype(jnp.bfloat16).reshape(2, channels, SUB, span)
                cross[:, :, pl.ds(first_bin, SUB), :] = product
            return 0

        lax.fori_loop(0, CHUNK // QUAD, one_quad, 0)

        def some_channels(number, _):
            first = number * ABREAST
            for part, table, total in ((0, cos_table, even), (1, sin_table, odd)):
                rows = jnp.concatenate([cross[part, first + i].T for i in range(ABREAST)], axis=0)
                result = jnp.dot(rows, table[chunk], preferred_element_type=jnp.float32)
                total[pl.ds(first, ABREAST)] += result.reshape(ABREAST, span, LAGS)
            return 0

        lax.fori_loop(0, channels // ABREAST, some_channels, 0)
        return 0

    lax.fori_loop(0, chunks, one_chunk, 0)

    for channel in range(channels):
        cos_sum = even[channel]
        sin_sum = odd[channel]
        lags[channel, :span, :] = (cos_sum - sin_sum).astype(jnp.bfloat16)
        back_sum = (cos_sum + sin_sum)[channels:]
        for half in range(LAGS // TILE):
            lanes = slice(half * TILE, (half + 1) * TILE)
            mirrored[half, pl.ds(channel, BLOCKS * channels, stride=channels), :] = back_sum[:, lanes]

    def travels(group, place):
        return place != LAST or group * few < EDGE

    def back(group, place):
        return pltpu.make_async_remote_copy(
            src_ref=back_out.at[group, place],
            dst_ref=lags.at[pl.ds(group * few, few), pl.ds(span + place * channels, channels), :],
            send_sem=back_send.at[group, place],
            recv_sem=back_recv.at[group, place],
            device_id={"chan": block(offset_of(place)), "win": win},
            device_id_type=MESH,
        )

    for group in range(GROUPS):
        for place in range(BLOCKS):
            if not travels(group, place):
                continue
            first = (place * channels + group * few) * channels
            for half in range(LAGS // TILE):
                rows = mirrored[half, first : first + few * channels].astype(jnp.bfloat16)
                lanes = slice(half * TILE, (half + 1) * TILE)
                back_out[group, place, :, :, lanes] = rows.reshape(few, channels, TILE)
            back(group, place).start()

    def slots_of(owner):
        return pl.ds(pl.multiple_of(owner * share, share), share)

    def to_core(group, half):
        return pltpu.make_async_remote_copy(
            src_ref=picked.at[pl.ds(group * few, few), slots_of(2 * half + 1 - core), :],
            dst_ref=from_core.at[half, pl.ds(group * few, few)],
            send_sem=core_send.at[group, half],
            recv_sem=core_recv.at[group, half],
            device_id={"chan": me, "win": other_core},
            device_id_type=MESH,
        )

    def away(group):
        return pltpu.make_async_remote_copy(
            src_ref=to_far.at[pl.ds(group * few, few)],
            dst_ref=from_far.at[pl.ds(group * few, few)],
            send_sem=far_send.at[group],
            recv_sem=far_recv.at[group],
            device_id={"chan": me, "win": other_far},
            device_id_type=MESH,
        )

    for group in range(GROUPS + 1):
        if group < GROUPS:
            for place in range(BLOCKS):
                if travels(group, place):
                    back(group, place).wait_recv()
            for channel in range(group * few, (group + 1) * few):
                rows = jnp.dot(chosen[channel], lags[channel], preferred_element_type=jnp.float32)
                picked[channel] = rows.astype(jnp.bfloat16)
            for half in range(2):
                to_core(group, half).start()
        if group > 0:
            for half in range(2):
                to_core(group - 1, half).wait_recv()
            for channel in range((group - 1) * few, group * few):
                mine = picked[channel, slots_of(other_far), :].astype(jnp.float32)
                theirs = from_core[1 - far, channel].astype(jnp.float32)
                to_far[channel] = (mine + theirs).astype(jnp.bfloat16)
            away(group - 1).start()
    scale = 1.0 / math.sqrt(windows * lax.axis_size("win") * bins)
    for group in range(GROUPS):
        away(group).wait_recv()
        for channel in range(group * few, (group + 1) * few):
            mine = picked[channel, slots_of(win), :].astype(jnp.float32)
            theirs = from_core[far, channel].astype(jnp.float32) + from_far[channel].astype(jnp.float32)
            for half in range(LAGS // TILE):
                lanes = slice(half * TILE, (half + 1) * TILE)
                out_ref[half, pl.ds(channel, share, stride=channels), :] = ((mine + theirs) * scale)[:, lanes]

    for chunk in range(chunks):
        for place in range(BLOCKS):
            halo(chunk, place).wait_send()
    for group in range(GROUPS):
        for place in range(BLOCKS):
            if travels(group, place):
                back(group, place).wait_send()
        for half in range(2):
            to_core(group, half).wait_send()
        away(group).wait_send()


def on_device(spectra, partners, pair_mask, gap_flags):
    _, windows, channels, bins = spectra.shape
    slots = partners.shape[1]
    chunks = bins // CHUNK
    span = (BLOCKS + 1) * channels
    share = slots // 4
    bf16 = jnp.bfloat16
    main, rest = bin_order()
    cos_table, sin_table = lag_tables(bins)
    anywhere = pl.BlockSpec(memory_space=pl.ANY)
    scalars = pl.BlockSpec(memory_space=pltpu.SMEM)
    semaphores = pltpu.SemaphoreType.DMA
    stacked = pl.pallas_call(
        kernel,
        out_shape=jax.ShapeDtypeStruct((LAGS // TILE, share * channels, TILE), jnp.float32),
        in_specs=[anywhere] * 3 + [scalars] + [anywhere] * 4,
        out_specs=pl.BlockSpec(memory_space=pltpu.VMEM),
        scratch_shapes=[
            pltpu.VMEM(spectra.shape, bf16),
            pltpu.VMEM(partners.shape, jnp.int32),
            pltpu.VMEM(pair_mask.shape, jnp.int32),
            pltpu.VMEM(main.shape, bf16),
            pltpu.VMEM(rest.shape, bf16),
            pltpu.VMEM(cos_table.shape, bf16),
            pltpu.VMEM(sin_table.shape, bf16),
            pltpu.VMEM((bins // TILE * channels, 2 * windows * TILE), bf16),
            pltpu.VMEM((chunks, channels, CHUNK_LANES), bf16),
            pltpu.VMEM((chunks, span, CHUNK_LANES), bf16),
            pltpu.VMEM((chunks, channels, QUAD_LANES), bf16),
            pltpu.VMEM((chunks, channels, QUAD_LANES), bf16),
            pltpu.VMEM((2, channels, CHUNK, span), bf16),
            pltpu.VMEM((channels, span, LAGS), jnp.float32),
            pltpu.VMEM((channels, span, LAGS), jnp.float32),
            pltpu.VMEM((channels, slots, 2 * span), bf16),
            pltpu.VMEM((LAGS // TILE, BLOCKS * channels * channels, TILE), jnp.float32),
            pltpu.VMEM((channels, 2 * span, LAGS), bf16),
            pltpu.VMEM((GROUPS, BLOCKS, channels // GROUPS, channels, LAGS), bf16),
            pltpu.VMEM((channels, slots, LAGS), bf16),
            pltpu.VMEM((2, channels, share, LAGS), bf16),
            pltpu.VMEM((channels, share, LAGS), bf16),
            pltpu.VMEM((channels, share, LAGS), bf16),
            semaphores((windows + 6,)),
            semaphores((chunks, BLOCKS)),
            semaphores((chunks, BLOCKS)),
            semaphores((GROUPS, BLOCKS)),
            semaphores((GROUPS, BLOCKS)),
            semaphores((GROUPS, 2)),
            semaphores((GROUPS, 2)),
            semaphores((GROUPS,)),
            semaphores((GROUPS,)),
        ],
        compiler_params=pltpu.CompilerParams(
            collective_id=0, has_side_effects=True, vmem_limit_bytes=56 * 2**20
        ),
        name="stack",
    )(spectra, partners, pair_mask, gap_flags, main, rest, cos_table, sin_table)
    stacked = stacked.reshape(LAGS // TILE, share, channels, TILE)
    return jnp.transpose(stacked, (1, 2, 0, 3)).reshape(share, channels, LAGS)


def solution(mesh):
    placed = (P(None, "win", "chan", None), P("chan", None), P("chan", None), P("chan"))
    return jax.shard_map(
        on_device, mesh=mesh, in_specs=placed, out_specs=P("win", "chan", None), check_vma=False
    )
```

```python
import functools
import math

import jax
import jax.numpy as jnp
import numpy as np
from jax import lax
from jax.experimental import pallas as pl
from jax.experimental.pallas import tpu as pltpu
from jax.sharding import PartitionSpec as P

LAGS = 256
SMOOTH = 8
FLO = 64
NSAMP = 6000
water_level = 0.1

MESH = pl.DeviceIdType.MESH
OFFSETS = (1, -2, 3, 4, -5, -6, 7)
BLOCKS = len(OFFSETS)
FIRST, SECOND = 1, 5
RELAY = OFFSETS[SECOND] - OFFSETS[FIRST]
NEXT, THIRD, ROW = 0, 2, 3
WIDE = 4
LAST = BLOCKS - 1
EDGE = 4
TILE = 128
SUB = 16
QUAD = 64
QUAD_LANES = 640
CHUNK = 256
CHUNK_LANES = CHUNK // QUAD * QUAD_LANES
EARLY = 4
RELAYED = 2
WINDOW = 2
GROUPS = 8
ABREAST = 16


def bin_order():
    main = np.zeros((8 * TILE, 8 * TILE), np.float32)
    part, f = np.meshgrid(np.arange(8), np.arange(TILE), indexing="ij")
    main[part * TILE + f, (f // SUB) * TILE + part * SUB + f % SUB] = 1.0
    rest = np.zeros((2 * TILE, 2 * TILE), np.float32)
    part, f = np.meshgrid(np.arange(2), np.arange(TILE), indexing="ij")
    rest[part * TILE + f, (f // QUAD) * TILE + part * QUAD + f % QUAD] = 1.0
    return main.astype(jnp.bfloat16), rest.astype(jnp.bfloat16)


def lag_tables(bins):
    steps = np.mod((FLO + np.arange(bins))[:, None] * (np.arange(LAGS) - LAGS // 2)[None, :], NSAMP)
    angles = steps.astype(np.float64) * (2.0 * math.pi / NSAMP)
    shape = (bins // CHUNK, CHUNK, LAGS)
    return (
        np.cos(angles).astype(np.float32).reshape(shape).astype(jnp.bfloat16),
        np.sin(angles).astype(np.float32).reshape(shape).astype(jnp.bfloat16),
    )


def kernel(
    spectra_ref, partners_ref, mask_ref, gap_ref, main_ref, rest_ref, cos_ref, sin_ref, out_ref,
    spectra, gap, partners, mask, main, rest, cos_table, sin_table,
    held, turned, around, edge_out, edge_in, cross, even, odd, chosen, mirrored, lags, back_out, picked, from_core, to_far, from_far,
    load_sem, halo_send, halo_recv, back_send, back_recv, core_send, core_recv, far_send, far_recv,
):
    windows, channels, bins = spectra.shape[1:]
    tiles = bins // TILE
    chunks = bins // CHUNK
    span = around.shape[1]
    slots = partners.shape[1]
    share = slots // 4
    few = channels // GROUPS
    count = lax.axis_size("chan")
    me = lax.axis_index("chan")
    win = lax.axis_index("win")
    core = lax.rem(win, 2)
    far = win // 2
    other_core = win + 1 - 2 * core
    other_far = lax.rem(win + 2, 4)

    side = 1 - 2 * core

    def offset_of(place):
        return OFFSETS[place] if place == LAST else side * OFFSETS[place]

    def block(offset):
        return lax.rem(me + count + offset, count)

    loads = [(gap_ref, gap), (spectra_ref.at[:, 0], spectra.at[:, 0])]
    loads += [(spectra_ref.at[:, window], spectra.at[:, window]) for window in range(1, windows)]
    loads += [(main_ref, main), (rest_ref, rest), (partners_ref, partners), (mask_ref, mask)]
    loads += [(cos_ref, cos_table), (sin_ref, sin_table)]
    loads = [pltpu.make_async_copy(source, target, load_sem.at[i]) for i, (source, target) in enumerate(loads)]
    for load in loads[: windows + 3]:
        load.start()
    barrier = pltpu.get_barrier_semaphore()
    for place in range(BLOCKS):
        for chan in (block(offset_of(place)), block(-offset_of(place))):
            pl.semaphore_signal(barrier, inc=1, device_id={"chan": chan, "win": win}, device_id_type=MESH)
    for partner in (other_core, other_far):
        pl.semaphore_signal(barrier, inc=1, device_id={"chan": me, "win": partner}, device_id_type=MESH)

    position = lax.broadcasted_iota(jnp.int32, (1, bins), 1)
    bin_count = jnp.minimum(position + SMOOTH, bins - 1) - jnp.maximum(position - SMOOTH, 0) + 1
    inverse = 1.0 / bin_count.astype(jnp.float32)
    loads[0].wait()
    row = lax.broadcasted_iota(jnp.int32, (channels, channels), 0)
    lane = lax.broadcasted_iota(jnp.int32, (channels, channels), 1)
    live = jnp.where((row == lane) & (gap[...] == 0), 1.0, 0.0)
    live = jnp.sum(live, axis=1, keepdims=True)
    pad = jnp.zeros((channels, TILE), jnp.float32)
    for window in range(windows):
        loads[window + 1].wait()
        real_part = spectra[0, window].astype(jnp.float32)
        imag_part = spectra[1, window].astype(jnp.float32)
        magnitude = jnp.sqrt(real_part * real_part + imag_part * imag_part)
        band_mean = jnp.sum(magnitude, axis=1, keepdims=True) * (1.0 / bins)
        padded = jnp.concatenate([magnitude, pad], axis=1)
        width = bins + TILE
        total = padded
        for step in (1, 2, 4, 8):
            total = total + pltpu.roll(total, step, 1)
        near = pltpu.roll(total, width - SMOOTH, 1) + pltpu.roll(padded, SMOOTH, 1)
        divisor = near[:, :bins] * inverse + water_level * band_mean + 1e-06
        factor = live / divisor
        white_real = (real_part * factor).astype(jnp.bfloat16)
        white_imag = (imag_part * factor).astype(jnp.bfloat16)
        for tile in range(tiles):
            rows = slice(tile * channels, (tile + 1) * channels)
            lanes = slice(tile * TILE, (tile + 1) * TILE)
            held[rows, 2 * window * TILE : (2 * window + 1) * TILE] = white_real[:, lanes]
            held[rows, (2 * window + 1) * TILE : (2 * window + 2) * TILE] = white_imag[:, lanes]

    def ordered(source, store):
        wide_first = jnp.dot(source[:, : 8 * TILE], main[...], preferred_element_type=jnp.float32)
        wide_last = jnp.dot(source[:, 8 * TILE :], rest[...], preferred_element_type=jnp.float32)
        first, last = wide_first.astype(jnp.bfloat16), wide_last.astype(jnp.bfloat16)
        for tile in range(tiles):
            rows = slice(tile * channels, (tile + 1) * channels)
            for half in range(2):
                quad = tile * 2 + half
                chunk, start = quad // (CHUNK // QUAD), quad % (CHUNK // QUAD) * QUAD_LANES
                store(chunk, slice(start, start + 4 * TILE), first[rows, half * 4 * TILE : (half + 1) * 4 * TILE])
                store(
                    chunk, slice(start + 4 * TILE, start + QUAD_LANES), last[rows, half * TILE : (half + 1) * TILE]
                )
        return wide_first, wide_last

    def store_around(chunk, lanes, value):
        around[chunk, :channels, lanes] = value

    def store_turned(chunk, lanes, value):
        turned[chunk, :, lanes] = value

    loads[windows + 1].wait()
    loads[windows + 2].wait()
    wide_first, wide_last = ordered(held[...], store_around)
    for chunk in range(chunks):
        pieces = []
        for quad in range(CHUNK // QUAD):
            tile, half = divmod(chunk * (CHUNK // QUAD) + quad, 2)
            rows = slice(tile * channels, tile * channels + EDGE)
            first = wide_first[rows, half * 4 * TILE : (half + 1) * 4 * TILE]
            last = wide_last[rows, half * TILE : (half + 1) * TILE]
            pieces.append(jnp.concatenate([first, last], axis=1))
        edge_out[chunk] = jnp.concatenate(pieces, axis=0).astype(jnp.bfloat16)

    def column_of(chan):
        x = lax.rem(chan, WIDE)
        return x + core * (WIDE - 1 - 2 * x)

    def halo(chunk, place, relayed=False):
        to, sent = block(-offset_of(place)), place
        if place == SECOND:
            to = block(-side * RELAY)
        if relayed:
            to, sent = block(side * (WIDE - OFFSETS[place])), BLOCKS + place // 2
        if place == LAST:
            source, target = edge_out.at[chunk], edge_in.at[chunk]
        else:
            first = (ROW + 1) * channels if relayed else (FIRST + 1) * channels if place == SECOND else 0
            source = around.at[chunk, pl.ds(first, channels), :]
            target = around.at[chunk, pl.ds((place + 1) * channels, channels), :]
        return pltpu.make_async_remote_copy(
            src_ref=source,
            dst_ref=target,
            send_sem=halo_send.at[chunk, sent],
            recv_sem=halo_recv.at[chunk, place],
            device_id={"chan": to, "win": win},
            device_id_type=MESH,
        )

    def at_places(act, relayed):
        for place in (NEXT, THIRD):
            to = block(side * (WIDE - OFFSETS[place]) if relayed else -offset_of(place))
            from_row = column_of(to) >= (WIDE - 1 if place == NEXT else 1)
            pl.when(from_row if relayed else jnp.logical_not(from_row))(functools.partial(act, place))

    pl.semaphore_wait(barrier, 2 * BLOCKS + 2)
    def send(chunk):
        at_places(lambda place: halo(chunk, place).start(), False)
        for place in range(BLOCKS):
            if place not in (FIRST, SECOND, NEXT, THIRD, ROW):
                halo(chunk, place).start()

    def send_early(chunk):
        halo(chunk, ROW).start()
        halo(chunk, FIRST).start()

    for chunk in range(min(EARLY, chunks)):
        send_early(chunk)
    for chunk in range(min(WINDOW, chunks)):
        send(chunk)
    for load in loads[windows + 3 :]:
        load.start()

    parts = held[...]
    swapped = [parts[:, (i ^ 1) * TILE : ((i ^ 1) + 1) * TILE] for i in range(2 * windows)]
    swapped = [-one if i % 2 else one for i, one in enumerate(swapped)]
    ordered(jnp.concatenate(swapped, axis=1), store_turned)
    even[...] = jnp.zeros_like(even)
    odd[...] = jnp.zeros_like(odd)
    lags[:, span + BLOCKS * channels :, :] = jnp.zeros((channels, channels, LAGS), jnp.bfloat16)
    lags[EDGE:, span + LAST * channels : span + BLOCKS * channels, :] = jnp.zeros(
        (channels - EDGE, channels, LAGS), jnp.bfloat16
    )

    loads[windows + 3].wait()
    loads[windows + 4].wait()
    lane = lax.broadcasted_iota(jnp.int32, (1, 2 * span), 1)
    column = lane
    for place in range(BLOCKS):
        offset = offset_of(place)
        column = jnp.where(lane // channels == place + 1, lane + (offset - place - 1) * channels, column)
        column = jnp.where(lane // channels == place + 1 + BLOCKS, lane - (offset + place + 1 + BLOCKS) * channels, column)
    column = jnp.where(lane // channels == 2 * BLOCKS + 1, 2**20, column).astype(jnp.float32)
    relative = jnp.where(mask[...] > 0, partners[...] - me * channels, -(2**20)).astype(jnp.float32)
    relative = jnp.concatenate([relative, jnp.zeros((TILE - channels, slots), jnp.float32)], axis=0).T
    for channel in range(channels):
        match = relative[:, channel : channel + 1] == column
        chosen[channel] = jnp.where(match, 1.0, 0.0).astype(jnp.bfloat16)

    row = lax.broadcasted_iota(jnp.int32, (SUB, TILE), 0)
    lane = lax.broadcasted_iota(jnp.int32, (SUB, TILE), 1)
    masks = []
    for group in range(QUAD // SUB):
        first = (lane % SUB == row).astype(jnp.float32)
        last = (lane % QUAD == group * SUB + row).astype(jnp.float32)
        masks.append(jnp.concatenate([first, last], axis=1).astype(jnp.bfloat16))
    loads[windows + 5].wait()
    loads[windows + 6].wait()

    def relay(chunk):
        halo(chunk, ROW).wait_recv()
        at_places(lambda place: halo(chunk, place, True).start(), True)
        halo(chunk, FIRST).wait_recv()
        halo(chunk, SECOND).start()

    for chunk in range(min(RELAYED, chunks)):
        relay(chunk)

    def one_chunk(chunk, _):
        @pl.when(chunk + RELAYED < chunks)
        def _():
            relay(chunk + RELAYED)

        @pl.when(chunk + EARLY < chunks)
        def _():
            send_early(chunk + EARLY)

        @pl.when(chunk + WINDOW < chunks)
        def _():
            send(chunk + WINDOW)

        for place in range(BLOCKS):
            if place not in (FIRST, ROW):
                halo(chunk, place).wait_recv()
        edge = edge_in[chunk].astype(jnp.float32)
        for quad in range(CHUNK // QUAD):
            shift = (channels - quad * EDGE) % channels
            rows = (pltpu.roll(edge, shift, 0) if shift else edge).astype(jnp.bfloat16)
            around[chunk, span - channels :, quad * QUAD_LANES : (quad + 1) * QUAD_LANES] = rows

        def one_quad(quad, _):
            start = pl.multiple_of(quad * QUAD_LANES, TILE)

            def lane_tiles(ref, rows, group):
                first = ref[chunk, :rows, pl.ds(pl.multiple_of(start + group * TILE, TILE), TILE)]
                last = ref[chunk, :rows, pl.ds(pl.multiple_of(start + 4 * TILE, TILE), TILE)]
                return jnp.concatenate([first, last], axis=1)

            for group in range(QUAD // SUB):
                others = lane_tiles(around, span, group)
                own = jnp.concatenate([lane_tiles(ref, channels, group) for ref in (around, turned)], axis=0)
                spread = (own[:, None, :] * masks[group][None, :, :]).reshape(2 * channels * SUB, 2 * TILE)
                product = lax.dot_general(
                    spread, others, (((1,), (1,)), ((), ())), preferred_element_type=jnp.float32
                )
                first_bin = pl.multiple_of(quad * QUAD + group * SUB, SUB)
                product = product.astype(jnp.bfloat16).reshape(2, channels, SUB, span)
                cross[:, :, pl.ds(first_bin, SUB), :] = product
            return 0

        lax.fori_loop(0, CHUNK // QUAD, one_quad, 0)

        def some_channels(number, _):
            first = number * ABREAST
            for part, table, total in ((0, cos_table, even), (1, sin_table, odd)):
                rows = jnp.concatenate([cross[part, first + i].T for i in range(ABREAST)], axis=0)
                result = jnp.dot(rows, table[chunk], preferred_element_type=jnp.float32)
                total[pl.ds(first, ABREAST)] += result.reshape(ABREAST, span, LAGS)
            return 0

        lax.fori_loop(0, channels // ABREAST, some_channels, 0)
        return 0

    lax.fori_loop(0, chunks, one_chunk, 0)

    for channel in range(channels):
        cos_sum = even[channel]
        sin_sum = odd[channel]
        lags[channel, :span, :] = (cos_sum - sin_sum).astype(jnp.bfloat16)
        back_sum = (cos_sum + sin_sum)[channels:]
        for half in range(LAGS // TILE):
            lanes = slice(half * TILE, (half + 1) * TILE)
            mirrored[half, pl.ds(channel, BLOCKS * channels, stride=channels), :] = back_sum[:, lanes]

    def travels(group, place):
        return place != LAST or group * few < EDGE

    def back(group, place):
        return pltpu.make_async_remote_copy(
            src_ref=back_out.at[group, place],
            dst_ref=lags.at[pl.ds(group * few, few), pl.ds(span + place * channels, channels), :],
            send_sem=back_send.at[group, place],
            recv_sem=back_recv.at[group, place],
            device_id={"chan": block(offset_of(place)), "win": win},
            device_id_type=MESH,
        )

    for group in range(GROUPS):
        for place in range(BLOCKS):
            if not travels(group, place):
                continue
            first = (place * channels + group * few) * channels
            for half in range(LAGS // TILE):
                rows = mirrored[half, first : first + few * channels].astype(jnp.bfloat16)
                lanes = slice(half * TILE, (half + 1) * TILE)
                back_out[group, place, :, :, lanes] = rows.reshape(few, channels, TILE)
            back(group, place).start()

    def slots_of(owner):
        return pl.ds(pl.multiple_of(owner * share, share), share)

    def to_core(group, half):
        return pltpu.make_async_remote_copy(
            src_ref=picked.at[pl.ds(group * few, few), slots_of(2 * half + 1 - core), :],
            dst_ref=from_core.at[half, pl.ds(group * few, few)],
            send_sem=core_send.at[group, half],
            recv_sem=core_recv.at[group, half],
            device_id={"chan": me, "win": other_core},
            device_id_type=MESH,
        )

    def away(group):
        return pltpu.make_async_remote_copy(
            src_ref=to_far.at[pl.ds(group * few, few)],
            dst_ref=from_far.at[pl.ds(group * few, few)],
            send_sem=far_send.at[group],
            recv_sem=far_recv.at[group],
            device_id={"chan": me, "win": other_far},
            device_id_type=MESH,
        )

    for group in range(GROUPS + 1):
        if group < GROUPS:
            for place in range(BLOCKS):
                if travels(group, place):
                    back(group, place).wait_recv()
            for channel in range(group * few, (group + 1) * few):
                rows = jnp.dot(chosen[channel], lags[channel], preferred_element_type=jnp.float32)
                picked[channel] = rows.astype(jnp.bfloat16)
            for half in range(2):
                to_core(group, half).start()
        if group > 0:
            for half in range(2):
                to_core(group - 1, half).wait_recv()
            for channel in range((group - 1) * few, group * few):
                mine = picked[channel, slots_of(other_far), :].astype(jnp.float32)
                theirs = from_core[1 - far, channel].astype(jnp.float32)
                to_far[channel] = (mine + theirs).astype(jnp.bfloat16)
            away(group - 1).start()
    scale = 1.0 / math.sqrt(windows * lax.axis_size("win") * bins)
    for group in range(GROUPS):
        away(group).wait_recv()
        for channel in range(group * few, (group + 1) * few):
            mine = picked[channel, slots_of(win), :].astype(jnp.float32)
            theirs = from_core[far, channel].astype(jnp.float32) + from_far[channel].astype(jnp.float32)
            for half in range(LAGS // TILE):
                lanes = slice(half * TILE, (half + 1) * TILE)
                out_ref[half, pl.ds(channel, share, stride=channels), :] = ((mine + theirs) * scale)[:, lanes]

    for chunk in range(chunks):
        for relayed in (False, True):
            at_places(lambda place, relayed=relayed: halo(chunk, place, relayed).wait_send(), relayed)
        for place in range(BLOCKS):
            if place not in (NEXT, THIRD):
                halo(chunk, place).wait_send()
    for group in range(GROUPS):
        for place in range(BLOCKS):
            if travels(group, place):
                back(group, place).wait_send()
        for half in range(2):
            to_core(group, half).wait_send()
        away(group).wait_send()


def on_device(spectra, partners, pair_mask, gap_flags):
    _, windows, channels, bins = spectra.shape
    slots = partners.shape[1]
    chunks = bins // CHUNK
    span = (BLOCKS + 1) * channels
    share = slots // 4
    bf16 = jnp.bfloat16
    main, rest = bin_order()
    cos_table, sin_table = lag_tables(bins)
    anywhere = pl.BlockSpec(memory_space=pl.ANY)
    semaphores = pltpu.SemaphoreType.DMA
    stacked = pl.pallas_call(
        kernel,
        out_shape=jax.ShapeDtypeStruct((LAGS // TILE, share * channels, TILE), jnp.float32),
        in_specs=[anywhere] * 8,
        out_specs=pl.BlockSpec(memory_space=pltpu.VMEM),
        scratch_shapes=[
            pltpu.VMEM(spectra.shape, bf16),
            pltpu.VMEM((1, channels), jnp.int32),
            pltpu.VMEM(partners.shape, jnp.int32),
            pltpu.VMEM(pair_mask.shape, jnp.int32),
            pltpu.VMEM(main.shape, bf16),
            pltpu.VMEM(rest.shape, bf16),
            pltpu.VMEM(cos_table.shape, bf16),
            pltpu.VMEM(sin_table.shape, bf16),
            pltpu.VMEM((bins // TILE * channels, 2 * windows * TILE), bf16),
            pltpu.VMEM((chunks, channels, CHUNK_LANES), bf16),
            pltpu.VMEM((chunks, span, CHUNK_LANES), bf16),
            pltpu.VMEM((chunks, channels, QUAD_LANES), bf16),
            pltpu.VMEM((chunks, channels, QUAD_LANES), bf16),
            pltpu.VMEM((2, channels, CHUNK, span), bf16),
            pltpu.VMEM((channels, span, LAGS), jnp.float32),
            pltpu.VMEM((channels, span, LAGS), jnp.float32),
            pltpu.VMEM((channels, slots, 2 * span), bf16),
            pltpu.VMEM((LAGS // TILE, BLOCKS * channels * channels, TILE), jnp.float32),
            pltpu.VMEM((channels, 2 * span, LAGS), bf16),
            pltpu.VMEM((GROUPS, BLOCKS, channels // GROUPS, channels, LAGS), bf16),
            pltpu.VMEM((channels, slots, LAGS), bf16),
            pltpu.VMEM((2, channels, share, LAGS), bf16),
            pltpu.VMEM((channels, share, LAGS), bf16),
            pltpu.VMEM((channels, share, LAGS), bf16),
            semaphores((windows + 7,)),
            semaphores((chunks, BLOCKS + 2)),
            semaphores((chunks, BLOCKS)),
            semaphores((GROUPS, BLOCKS)),
            semaphores((GROUPS, BLOCKS)),
            semaphores((GROUPS, 2)),
            semaphores((GROUPS, 2)),
            semaphores((GROUPS,)),
            semaphores((GROUPS,)),
        ],
        compiler_params=pltpu.CompilerParams(
            collective_id=0, has_side_effects=True, vmem_limit_bytes=56 * 2**20
        ),
        name="stack",
    )(spectra, partners, pair_mask, gap_flags[None, :], main, rest, cos_table, sin_table)
    stacked = stacked.reshape(LAGS // TILE, share, channels, TILE)
    return jnp.transpose(stacked, (1, 2, 0, 3)).reshape(share, channels, LAGS)


def solution(mesh):
    placed = (P(None, "win", "chan", None), P("chan", None), P("chan", None), P("chan"))
    return jax.shard_map(
        on_device, mesh=mesh, in_specs=placed, out_specs=P("win", "chan", None), check_vma=False
    )
```

```python
import functools
import math

import jax
import jax.numpy as jnp
import numpy as np
from jax import lax
from jax.experimental import pallas as pl
from jax.experimental.pallas import tpu as pltpu
from jax.sharding import PartitionSpec as P

LAGS = 256
SMOOTH = 8
FLO = 64
NSAMP = 6000
water_level = 0.1

MESH = pl.DeviceIdType.MESH
OFFSETS = (1, -2, 3, 4, -5, -6, 7)
BLOCKS = len(OFFSETS)
FIRST, SECOND = 1, 5
RELAY = OFFSETS[SECOND] - OFFSETS[FIRST]
NEXT, THIRD, ROW = 0, 2, 3
WIDE = 4
LAST = BLOCKS - 1
EDGE = 4
TILE = 128
SUB = 16
QUAD = 64
QUAD_LANES = 640
CHUNK = 256
CHUNK_LANES = CHUNK // QUAD * QUAD_LANES
EARLY = 4
RELAYED = 2
WINDOW = 2
GROUPS = 8
ABREAST = 16


def bin_order():
    main = np.zeros((8 * TILE, 8 * TILE), np.float32)
    part, f = np.meshgrid(np.arange(8), np.arange(TILE), indexing="ij")
    main[part * TILE + f, (f // SUB) * TILE + part * SUB + f % SUB] = 1.0
    rest = np.zeros((2 * TILE, 2 * TILE), np.float32)
    part, f = np.meshgrid(np.arange(2), np.arange(TILE), indexing="ij")
    rest[part * TILE + f, (f // QUAD) * TILE + part * QUAD + f % QUAD] = 1.0
    return main.astype(jnp.bfloat16), rest.astype(jnp.bfloat16)


def lag_tables(bins):
    steps = np.mod((FLO + np.arange(bins))[:, None] * (np.arange(LAGS) - LAGS // 2)[None, :], NSAMP)
    angles = steps.astype(np.float64) * (2.0 * math.pi / NSAMP)
    shape = (bins // CHUNK, CHUNK, LAGS)
    return (
        np.cos(angles).astype(np.float32).reshape(shape).astype(jnp.bfloat16),
        np.sin(angles).astype(np.float32).reshape(shape).astype(jnp.bfloat16),
    )


def kernel(
    spectra_ref, partners_ref, mask_ref, gap_ref, main_ref, rest_ref, cos_ref, sin_ref, out_ref,
    spectra, gap, partners, mask, main, rest, cos_table, sin_table,
    held, turned, around, edge_out, edge_in, cross, even, odd, chosen, mirrored, lags, back_out, picked, from_core, to_far, from_far,
    load_sem, halo_send, halo_recv, back_send, back_recv, core_send, core_recv, far_send, far_recv,
):
    windows, channels, bins = spectra.shape[1:]
    tiles = bins // TILE
    chunks = bins // CHUNK
    span = around.shape[1]
    slots = partners.shape[1]
    share = slots // 4
    few = channels // GROUPS
    count = lax.axis_size("chan")
    me = lax.axis_index("chan")
    win = lax.axis_index("win")
    core = lax.rem(win, 2)
    far = win // 2
    other_core = win + 1 - 2 * core
    other_far = lax.rem(win + 2, 4)

    side = 1 - 2 * core

    def offset_of(place):
        return OFFSETS[place] if place == LAST else side * OFFSETS[place]

    def block(offset):
        return lax.rem(me + count + offset, count)

    loads = [(gap_ref, gap), (spectra_ref.at[:, 0], spectra.at[:, 0])]
    loads += [(spectra_ref.at[:, window], spectra.at[:, window]) for window in range(1, windows)]
    loads += [(main_ref, main), (rest_ref, rest), (partners_ref, partners), (mask_ref, mask)]
    loads += [(cos_ref, cos_table), (sin_ref, sin_table)]
    loads = [pltpu.make_async_copy(source, target, load_sem.at[i]) for i, (source, target) in enumerate(loads)]
    for load in loads[: windows + 3]:
        load.start()
    barrier = pltpu.get_barrier_semaphore()
    for place in range(BLOCKS):
        for chan in (block(offset_of(place)), block(-offset_of(place))):
            pl.semaphore_signal(barrier, inc=1, device_id={"chan": chan, "win": win}, device_id_type=MESH)
    for partner in (other_core, other_far):
        pl.semaphore_signal(barrier, inc=1, device_id={"chan": me, "win": partner}, device_id_type=MESH)

    position = lax.broadcasted_iota(jnp.int32, (1, bins), 1)
    bin_count = jnp.minimum(position + SMOOTH, bins - 1) - jnp.maximum(position - SMOOTH, 0) + 1
    inverse = 1.0 / bin_count.astype(jnp.float32)
    loads[0].wait()
    row = lax.broadcasted_iota(jnp.int32, (channels, channels), 0)
    lane = lax.broadcasted_iota(jnp.int32, (channels, channels), 1)
    live = jnp.where((row == lane) & (gap[...] == 0), 1.0, 0.0)
    live = jnp.sum(live, axis=1, keepdims=True)
    pad = jnp.zeros((channels, TILE), jnp.float32)
    for window in range(windows):
        loads[window + 1].wait()
        real_part = spectra[0, window].astype(jnp.float32)
        imag_part = spectra[1, window].astype(jnp.float32)
        magnitude = jnp.sqrt(real_part * real_part + imag_part * imag_part)
        band_mean = jnp.sum(magnitude, axis=1, keepdims=True) * (1.0 / bins)
        padded = jnp.concatenate([magnitude, pad], axis=1)
        width = bins + TILE
        total = padded
        for step in (1, 2, 4, 8):
            total = total + pltpu.roll(total, step, 1)
        near = pltpu.roll(total, width - SMOOTH, 1) + pltpu.roll(padded, SMOOTH, 1)
        divisor = near[:, :bins] * inverse + water_level * band_mean + 1e-06
        factor = live / divisor
        white_real = (real_part * factor).astype(jnp.bfloat16)
        white_imag = (imag_part * factor).astype(jnp.bfloat16)
        for tile in range(tiles):
            rows = slice(tile * channels, (tile + 1) * channels)
            lanes = slice(tile * TILE, (tile + 1) * TILE)
            held[rows, 2 * window * TILE : (2 * window + 1) * TILE] = white_real[:, lanes]
            held[rows, (2 * window + 1) * TILE : (2 * window + 2) * TILE] = white_imag[:, lanes]

    def ordered(source, store):
        wide_first = jnp.dot(source[:, : 8 * TILE], main[...], preferred_element_type=jnp.float32)
        wide_last = jnp.dot(source[:, 8 * TILE :], rest[...], preferred_element_type=jnp.float32)
        first, last = wide_first.astype(jnp.bfloat16), wide_last.astype(jnp.bfloat16)
        for tile in range(tiles):
            rows = slice(tile * channels, (tile + 1) * channels)
            for half in range(2):
                quad = tile * 2 + half
                chunk, start = quad // (CHUNK // QUAD), quad % (CHUNK // QUAD) * QUAD_LANES
                store(chunk, slice(start, start + 4 * TILE), first[rows, half * 4 * TILE : (half + 1) * 4 * TILE])
                store(
                    chunk, slice(start + 4 * TILE, start + QUAD_LANES), last[rows, half * TILE : (half + 1) * TILE]
                )
        return wide_first, wide_last

    def store_around(chunk, lanes, value):
        around[chunk, :channels, lanes] = value

    def store_turned(chunk, lanes, value):
        turned[chunk, :, lanes] = value

    loads[windows + 1].wait()
    loads[windows + 2].wait()
    wide_first, wide_last = ordered(held[...], store_around)
    for chunk in range(chunks):
        pieces = []
        for quad in range(CHUNK // QUAD):
            tile, half = divmod(chunk * (CHUNK // QUAD) + quad, 2)
            rows = slice(tile * channels, tile * channels + EDGE)
            first = wide_first[rows, half * 4 * TILE : (half + 1) * 4 * TILE]
            last = wide_last[rows, half * TILE : (half + 1) * TILE]
            pieces.append(jnp.concatenate([first, last], axis=1))
        edge_out[chunk] = jnp.concatenate(pieces, axis=0).astype(jnp.bfloat16)

    def column_of(chan):
        x = lax.rem(chan, WIDE)
        return x + core * (WIDE - 1 - 2 * x)

    def halo(chunk, place, relayed=False):
        to, sent = block(-offset_of(place)), place
        if place == SECOND:
            to = block(-side * RELAY)
        if relayed:
            to, sent = block(side * (WIDE - OFFSETS[place])), BLOCKS + place // 2
        if place == LAST:
            source, target = edge_out.at[chunk], edge_in.at[chunk]
        else:
            first = (ROW + 1) * channels if relayed else (FIRST + 1) * channels if place == SECOND else 0
            source = around.at[chunk, pl.ds(first, channels), :]
            target = around.at[chunk, pl.ds((place + 1) * channels, channels), :]
        return pltpu.make_async_remote_copy(
            src_ref=source,
            dst_ref=target,
            send_sem=halo_send.at[chunk, sent],
            recv_sem=halo_recv.at[chunk, place],
            device_id={"chan": to, "win": win},
            device_id_type=MESH,
        )

    def at_places(act, relayed):
        for place in (NEXT, THIRD):
            to = block(side * (WIDE - OFFSETS[place]) if relayed else -offset_of(place))
            from_row = column_of(to) >= (WIDE - 1 if place == NEXT else 1)
            pl.when(from_row if relayed else jnp.logical_not(from_row))(functools.partial(act, place))

    pl.semaphore_wait(barrier, 2 * BLOCKS + 2)
    def send(chunk):
        at_places(lambda place: halo(chunk, place).start(), False)
        for place in range(BLOCKS):
            if place not in (FIRST, SECOND, NEXT, THIRD, ROW):
                halo(chunk, place).start()

    def send_early(chunk):
        halo(chunk, ROW).start()
        halo(chunk, FIRST).start()

    for chunk in range(min(EARLY, chunks)):
        send_early(chunk)
    for chunk in range(min(WINDOW, chunks)):
        send(chunk)
    for load in loads[windows + 3 :]:
        load.start()

    parts = held[...]
    swapped = [parts[:, (i ^ 1) * TILE : ((i ^ 1) + 1) * TILE] for i in range(2 * windows)]
    swapped = [-one if i % 2 else one for i, one in enumerate(swapped)]
    ordered(jnp.concatenate(swapped, axis=1), store_turned)
    even[...] = jnp.zeros_like(even)
    odd[...] = jnp.zeros_like(odd)
    lags[:, span + BLOCKS * channels :, :] = jnp.zeros((channels, channels, LAGS), jnp.bfloat16)
    lags[EDGE:, span + LAST * channels : span + BLOCKS * channels, :] = jnp.zeros(
        (channels - EDGE, channels, LAGS), jnp.bfloat16
    )

    loads[windows + 3].wait()
    loads[windows + 4].wait()
    lane = lax.broadcasted_iota(jnp.int32, (1, 2 * span), 1)
    column = lane
    for place in range(BLOCKS):
        offset = offset_of(place)
        column = jnp.where(lane // channels == place + 1, lane + (offset - place - 1) * channels, column)
        column = jnp.where(lane // channels == place + 1 + BLOCKS, lane - (offset + place + 1 + BLOCKS) * channels, column)
    column = jnp.where(lane // channels == 2 * BLOCKS + 1, 2**20, column).astype(jnp.float32)
    relative = jnp.where(mask[...] > 0, partners[...] - me * channels, -(2**20)).astype(jnp.float32)
    relative = jnp.concatenate([relative, jnp.zeros((TILE - channels, slots), jnp.float32)], axis=0).T
    for channel in range(channels):
        match = relative[:, channel : channel + 1] == column
        chosen[channel] = jnp.where(match, 1.0, 0.0).astype(jnp.bfloat16)

    row = lax.broadcasted_iota(jnp.int32, (SUB, TILE), 0)
    lane = lax.broadcasted_iota(jnp.int32, (SUB, TILE), 1)
    masks = []
    for group in range(QUAD // SUB):
        first = (lane % SUB == row).astype(jnp.float32)
        last = (lane % QUAD == group * SUB + row).astype(jnp.float32)
        masks.append(jnp.concatenate([first, last], axis=1).astype(jnp.bfloat16))
    loads[windows + 5].wait()
    loads[windows + 6].wait()

    def relay(chunk):
        halo(chunk, ROW).wait_recv()
        at_places(lambda place: halo(chunk, place, True).start(), True)
        halo(chunk, FIRST).wait_recv()
        halo(chunk, SECOND).start()

    for chunk in range(min(RELAYED, chunks)):
        relay(chunk)

    def one_chunk(chunk, _):
        @pl.when(chunk + WINDOW < chunks)
        def _():
            send(chunk + WINDOW)

        @pl.when(chunk + EARLY < chunks)
        def _():
            send_early(chunk + EARLY)

        @pl.when(chunk + RELAYED < chunks)
        def _():
            relay(chunk + RELAYED)

        for place in range(BLOCKS):
            if place not in (FIRST, ROW):
                halo(chunk, place).wait_recv()
        edge = edge_in[chunk].astype(jnp.float32)
        for quad in range(CHUNK // QUAD):
            shift = (channels - quad * EDGE) % channels
            rows = (pltpu.roll(edge, shift, 0) if shift else edge).astype(jnp.bfloat16)
            around[chunk, span - channels :, quad * QUAD_LANES : (quad + 1) * QUAD_LANES] = rows

        def one_quad(quad, _):
            start = pl.multiple_of(quad * QUAD_LANES, TILE)

            def lane_tiles(ref, rows, group):
                first = ref[chunk, :rows, pl.ds(pl.multiple_of(start + group * TILE, TILE), TILE)]
                last = ref[chunk, :rows, pl.ds(pl.multiple_of(start + 4 * TILE, TILE), TILE)]
                return jnp.concatenate([first, last], axis=1)

            for group in range(QUAD // SUB):
                others = lane_tiles(around, span, group)
                own = jnp.concatenate([lane_tiles(ref, channels, group) for ref in (around, turned)], axis=0)
                spread = (own[:, None, :] * masks[group][None, :, :]).reshape(2 * channels * SUB, 2 * TILE)
                product = lax.dot_general(
                    spread, others, (((1,), (1,)), ((), ())), preferred_element_type=jnp.float32
                )
                first_bin = pl.multiple_of(quad * QUAD + group * SUB, SUB)
                product = product.astype(jnp.bfloat16).reshape(2, channels, SUB, span)
                cross[:, :, pl.ds(first_bin, SUB), :] = product
            return 0

        lax.fori_loop(0, CHUNK // QUAD, one_quad, 0)

        def some_channels(number, _):
            first = number * ABREAST
            for part, table, total in ((0, cos_table, even), (1, sin_table, odd)):
                rows = jnp.concatenate([cross[part, first + i].T for i in range(ABREAST)], axis=0)
                result = jnp.dot(rows, table[chunk], preferred_element_type=jnp.float32)
                total[pl.ds(first, ABREAST)] += result.reshape(ABREAST, span, LAGS)
            return 0

        lax.fori_loop(0, channels // ABREAST, some_channels, 0)
        return 0

    lax.fori_loop(0, chunks, one_chunk, 0)

    for channel in range(channels):
        cos_sum = even[channel]
        sin_sum = odd[channel]
        lags[channel, :span, :] = (cos_sum - sin_sum).astype(jnp.bfloat16)
        back_sum = (cos_sum + sin_sum)[channels:]
        for half in range(LAGS // TILE):
            lanes = slice(half * TILE, (half + 1) * TILE)
            mirrored[half, pl.ds(channel, BLOCKS * channels, stride=channels), :] = back_sum[:, lanes]

    def travels(group, place):
        return place != LAST or group * few < EDGE

    def back(group, place):
        return pltpu.make_async_remote_copy(
            src_ref=back_out.at[group, place],
            dst_ref=lags.at[pl.ds(group * few, few), pl.ds(span + place * channels, channels), :],
            send_sem=back_send.at[group, place],
            recv_sem=back_recv.at[group, place],
            device_id={"chan": block(offset_of(place)), "win": win},
            device_id_type=MESH,
        )

    longest_first = (SECOND, FIRST, LAST, 4, THIRD, NEXT, ROW)
    for group in range(GROUPS):
        for place in longest_first:
            if not travels(group, place):
                continue
            first = (place * channels + group * few) * channels
            for half in range(LAGS // TILE):
                rows = mirrored[half, first : first + few * channels].astype(jnp.bfloat16)
                lanes = slice(half * TILE, (half + 1) * TILE)
                back_out[group, place, :, :, lanes] = rows.reshape(few, channels, TILE)
            back(group, place).start()

    def slots_of(owner):
        return pl.ds(pl.multiple_of(owner * share, share), share)

    def to_core(group, half):
        return pltpu.make_async_remote_copy(
            src_ref=picked.at[pl.ds(group * few, few), slots_of(2 * half + 1 - core), :],
            dst_ref=from_core.at[half, pl.ds(group * few, few)],
            send_sem=core_send.at[group, half],
            recv_sem=core_recv.at[group, half],
            device_id={"chan": me, "win": other_core},
            device_id_type=MESH,
        )

    def away(group):
        return pltpu.make_async_remote_copy(
            src_ref=to_far.at[pl.ds(group * few, few)],
            dst_ref=from_far.at[pl.ds(group * few, few)],
            send_sem=far_send.at[group],
            recv_sem=far_recv.at[group],
            device_id={"chan": me, "win": other_far},
            device_id_type=MESH,
        )

    for group in range(GROUPS + 1):
        if group < GROUPS:
            for place in range(BLOCKS):
                if travels(group, place):
                    back(group, place).wait_recv()
            for channel in range(group * few, (group + 1) * few):
                rows = jnp.dot(chosen[channel], lags[channel], preferred_element_type=jnp.float32)
                picked[channel] = rows.astype(jnp.bfloat16)
            for half in range(2):
                to_core(group, half).start()
        if group > 0:
            for half in range(2):
                to_core(group - 1, half).wait_recv()
            for channel in range((group - 1) * few, group * few):
                mine = picked[channel, slots_of(other_far), :].astype(jnp.float32)
                theirs = from_core[1 - far, channel].astype(jnp.float32)
                to_far[channel] = (mine + theirs).astype(jnp.bfloat16)
            away(group - 1).start()
    scale = 1.0 / math.sqrt(windows * lax.axis_size("win") * bins)
    for group in range(GROUPS):
        away(group).wait_recv()
        for channel in range(group * few, (group + 1) * few):
            mine = picked[channel, slots_of(win), :].astype(jnp.float32)
            theirs = from_core[far, channel].astype(jnp.float32) + from_far[channel].astype(jnp.float32)
            for half in range(LAGS // TILE):
                lanes = slice(half * TILE, (half + 1) * TILE)
                out_ref[half, pl.ds(channel, share, stride=channels), :] = ((mine + theirs) * scale)[:, lanes]

    for chunk in range(chunks):
        for relayed in (False, True):
            at_places(lambda place, relayed=relayed: halo(chunk, place, relayed).wait_send(), relayed)
        for place in range(BLOCKS):
            if place not in (NEXT, THIRD):
                halo(chunk, place).wait_send()
    for group in range(GROUPS):
        for place in range(BLOCKS):
            if travels(group, place):
                back(group, place).wait_send()
        for half in range(2):
            to_core(group, half).wait_send()
        away(group).wait_send()


def on_device(spectra, partners, pair_mask, gap_flags):
    _, windows, channels, bins = spectra.shape
    slots = partners.shape[1]
    chunks = bins // CHUNK
    span = (BLOCKS + 1) * channels
    share = slots // 4
    bf16 = jnp.bfloat16
    main, rest = bin_order()
    cos_table, sin_table = lag_tables(bins)
    anywhere = pl.BlockSpec(memory_space=pl.ANY)
    semaphores = pltpu.SemaphoreType.DMA
    stacked = pl.pallas_call(
        kernel,
        out_shape=jax.ShapeDtypeStruct((LAGS // TILE, share * channels, TILE), jnp.float32),
        in_specs=[anywhere] * 8,
        out_specs=pl.BlockSpec(memory_space=pltpu.VMEM),
        scratch_shapes=[
            pltpu.VMEM(spectra.shape, bf16),
            pltpu.VMEM((1, channels), jnp.int32),
            pltpu.VMEM(partners.shape, jnp.int32),
            pltpu.VMEM(pair_mask.shape, jnp.int32),
            pltpu.VMEM(main.shape, bf16),
            pltpu.VMEM(rest.shape, bf16),
            pltpu.VMEM(cos_table.shape, bf16),
            pltpu.VMEM(sin_table.shape, bf16),
            pltpu.VMEM((bins // TILE * channels, 2 * windows * TILE), bf16),
            pltpu.VMEM((chunks, channels, CHUNK_LANES), bf16),
            pltpu.VMEM((chunks, span, CHUNK_LANES), bf16),
            pltpu.VMEM((chunks, channels, QUAD_LANES), bf16),
            pltpu.VMEM((chunks, channels, QUAD_LANES), bf16),
            pltpu.VMEM((2, channels, CHUNK, span), bf16),
            pltpu.VMEM((channels, span, LAGS), jnp.float32),
            pltpu.VMEM((channels, span, LAGS), jnp.float32),
            pltpu.VMEM((channels, slots, 2 * span), bf16),
            pltpu.VMEM((LAGS // TILE, BLOCKS * channels * channels, TILE), jnp.float32),
            pltpu.VMEM((channels, 2 * span, LAGS), bf16),
            pltpu.VMEM((GROUPS, BLOCKS, channels // GROUPS, channels, LAGS), bf16),
            pltpu.VMEM((channels, slots, LAGS), bf16),
            pltpu.VMEM((2, channels, share, LAGS), bf16),
            pltpu.VMEM((channels, share, LAGS), bf16),
            pltpu.VMEM((channels, share, LAGS), bf16),
            semaphores((windows + 7,)),
            semaphores((chunks, BLOCKS + 2)),
            semaphores((chunks, BLOCKS)),
            semaphores((GROUPS, BLOCKS)),
            semaphores((GROUPS, BLOCKS)),
            semaphores((GROUPS, 2)),
            semaphores((GROUPS, 2)),
            semaphores((GROUPS,)),
            semaphores((GROUPS,)),
        ],
        compiler_params=pltpu.CompilerParams(
            collective_id=0, has_side_effects=True, vmem_limit_bytes=56 * 2**20
        ),
        name="stack",
    )(spectra, partners, pair_mask, gap_flags[None, :], main, rest, cos_table, sin_table)
    stacked = stacked.reshape(LAGS // TILE, share, channels, TILE)
    return jnp.transpose(stacked, (1, 2, 0, 3)).reshape(share, channels, LAGS)


def solution(mesh):
    placed = (P(None, "win", "chan", None), P("chan", None), P("chan", None), P("chan"))
    return jax.shard_map(
        on_device, mesh=mesh, in_specs=placed, out_specs=P("win", "chan", None), check_vma=False
    )
```
